256 devices in a mesh: azim: 32 (over z, y_lo, core), radax: 8 (over y_hi, x).
Axes of the slice: x: 4, y: 4 (y_hi: 2, y_lo: 2; y = y_hi * 2 + y_lo), z: 8, core: 2. Of those that a mesh axis runs over, the one named last changes fastest.
Arguments:
- solution: float32 [256, 64, 16, 320], P('azim', 'radax'), may hold values from -6 to 6
- metric: float32 [256, 64, 16, 3], P('azim', 'radax'), may hold values from 1 to 4
- intersections: int32 [32, 2, 3, 8], P('azim'), may hold values from 0 to 15, as said below
- counts: int32 [32, 2], P('azim'), may hold values from 4 to 8, as said below
- projections: float32 [4, 16, 4, 4], replicated, may hold values from -3 to 3
Outputs:
- advanced: float32 [256, 64, 16, 320], P('azim', 'radax')
The draws below stay inside these ranges and needn't reach their ends.
Inputs may be any that keep to these rules, and one draw needn't show every extreme that they name: intersections[s, b] holds 8 slots of (rotor face's azimuthal index within sector (s - 1 + b) mod 32, stator face's azimuthal index within sector s, segment kind); face indices are below 8, kinds below 16; slots at or after counts[s, b] are padding. `counts`: used slots of each list; some sector fills its first list, some sector its second.
All inputs are finite; a program needn't handle non-finite values.
Results may differ from the reference program's by a relative error of at most 0.0001.
Values sent between devices are 32-bit elements; how exact they have to be, the bound alone decides.
No kernel may reach another device: no remote copies, remote signals or barrier semaphores. Data moves between devices by JAX's collectives and lax.ppermute only.
A program may use at most 128 MiB of HBM per device.

```python
import math
import jax
import jax.numpy as jnp
import numpy as np
from jax import lax

EA = 8
EX = 16
FIELDS = 5
NODES = 64
KINDS = 16
CAP = 8
NA = 256
NR = 64
N_AZIM = 32


def draw_intersections(key, part):
    key = jax.random.fold_in(key, 11)
    subkeys = jax.random.split(key, 4)
    rotor_side = jax.random.randint(subkeys[0], (N_AZIM, 2, 1, CAP), 0, EA)
    stator_side = jax.random.randint(subkeys[1], (N_AZIM, 2, 1, CAP), 0, EA)
    segment_kind = jax.random.randint(subkeys[2], (N_AZIM, 2, 1, CAP), 0, KINDS)
    entries = jnp.concatenate([rotor_side, stator_side, segment_kind], axis=2).astype(jnp.int32)
    chosen = jax.random.randint(subkeys[3], (), 0, N_AZIM)
    extremes = jnp.array([EA - 1, 0, KINDS - 1], jnp.int32)
    return entries.at[chosen, 0, :, 0].set(extremes)


def draw_counts(key, part):
    key = jax.random.fold_in(key, 23)
    subkeys = jax.random.split(key, 3)
    filled = jax.random.randint(subkeys[0], (N_AZIM, 2), CAP // 2, CAP + 1)
    fullest = jax.random.randint(subkeys[1], (), 0, N_AZIM)
    offset = jax.random.randint(subkeys[2], (), 1, N_AZIM)
    second = (fullest + offset) % N_AZIM
    filled = filled.at[fullest, 1].set(CAP // 2)
    filled = filled.at[fullest, 0].set(CAP)
    filled = filled.at[second, 1].set(CAP)
    return filled.astype(jnp.int32)


def block_levels(key, dims, cuts, low, high):
    def one(dim, blocks):
        draws = jax.random.uniform(jax.random.fold_in(jax.random.fold_in(key, 6), dim), (blocks,), jnp.float32, low / len(cuts), high / len(cuts))
        return jnp.repeat(jnp.exp(draws), dims[dim] // blocks).reshape((-1,) + (1,) * (len(dims) - dim - 1))

    level = one(*cuts[0])
    for cut in cuts[1:]:
        level = level * one(*cut)
    return level


def scatter_about(rng, dims, scale, most, cuts=(), kind=jnp.bfloat16):
    values = scale * jax.random.normal(rng, dims, jnp.float32)
    if cuts:
        values = values * block_levels(rng, dims, cuts, -0.22, 0.18)
    return jnp.clip(values, -most, most).astype(kind)


def setup_inputs(seed: int = 0) -> dict:
    keys = jax.random.split(jax.random.key(seed), 6)
    return {
        "solution": scatter_about(keys[0], (NA, NR, EX, FIELDS * NODES), 1.0, 6.0, ((0, 32), (1, 8)), jnp.float32),
        "metric": jnp.clip(jnp.exp(math.log(4.0) - 1.3862944 * jax.random.uniform(keys[1], (NA, NR, EX, 3), jnp.float32) ** block_levels(keys[1], (NA, NR, EX, 3), ((0, 32), (1, 8)), -0.2, 0.2)), 1.0, 4.0),
        "intersections": draw_intersections(jax.random.fold_in(keys[5], 71), 0),
        "counts": draw_counts(jax.random.fold_in(keys[5], 71), 0),
        "projections": scatter_about(keys[4], (4, KINDS, 4, 4), 0.5, 3.0, (), jnp.float32),
    }


time_step = 0.02
mean_flow = (0.5, 0.0, 0.4)
highest = lax.Precision.HIGHEST

def derivative_table():
    points = np.array([-1.0, -1.0 / np.sqrt(5.0), 1.0 / np.sqrt(5.0), 1.0])
    barycentric = np.array([1.0 / np.prod([points[j] - points[k] for k in range(4) if k != j]) for j in range(4)])
    single = np.zeros((4, 4))
    for i in range(4):
        for j in range(4):
            if i != j:
                single[i, j] = barycentric[j] / barycentric[i] / (points[i] - points[j])
        single[i, i] = -np.sum(single[i])
    identity = np.eye(4)
    along_first = np.kron(np.kron(single, identity), identity)
    along_second = np.kron(np.kron(identity, single), identity)
    along_third = np.kron(np.kron(identity, identity), single)
    return jnp.asarray(np.concatenate([along_first.T, along_second.T, along_third.T], axis=1), jnp.float32)

def flux_tables():
    jacobians = np.zeros((3, 5, 5))
    for d in range(3):
        jacobians[d] = np.eye(5) * mean_flow[d]
        jacobians[d, 0, 1 + d] += 1.0
        jacobians[d, 1 + d, 4] += 1.0
        jacobians[d, 4, 1 + d] += 1.0
    speeds = np.abs(np.array(mean_flow)) + 1.0
    lower_side = np.stack([speeds[d] * np.eye(5) + jacobians[d] for d in range(3)])
    upper_side = np.stack([speeds[d] * np.eye(5) - jacobians[d] for d in range(3)])
    return (jnp.asarray(jacobians, jnp.float32), jnp.asarray(lower_side, jnp.float32), jnp.asarray(upper_side, jnp.float32))

def volume_term(solution, metric, derivative, jacobians):
    leading = solution.shape[:-1]
    slopes = jnp.dot(solution.reshape(-1, 64), derivative, precision=highest).reshape(leading + (5, 3, 64))
    summed = jnp.einsum('...gdn,dfg,...d->...fn', slopes, jacobians, metric, precision=highest)
    return -summed.reshape(leading + (320,))

def face_term(coefficients, outside, inside, metric_scale):
    mixed = jnp.einsum('fg,...gjk->...fjk', coefficients, outside - inside, precision=highest)
    return 3.0 * metric_scale[..., None, None, None] * mixed

def place_faces(low_term, high_term, node_axis):
    low_part = jnp.expand_dims(low_term, node_axis)
    high_part = jnp.expand_dims(high_term, node_axis)
    filler = jnp.zeros_like(low_part)
    return jnp.concatenate([low_part, filler, filler, high_part], axis=node_axis)

def inside_traces(nodal):
    lows = [lax.index_in_dim(nodal, 0, node_axis, keepdims=False) for node_axis in (-3, -2, -1)]
    highs = [lax.index_in_dim(nodal, 3, node_axis, keepdims=False) for node_axis in (-3, -2, -1)]
    return (lows, highs)

def surface(nodal, metric, lows, highs, outside_first, outside_second, mortar_stator, mortar_rotor, lower_side, upper_side):
    layers = nodal.shape[2]
    middle = layers // 2
    zero_rim = jnp.zeros_like(highs[2][:, :, :1])
    outside_third = (jnp.concatenate([zero_rim, highs[2][:, :, :-1]], axis=2), jnp.concatenate([lows[2][:, :, 1:], zero_rim], axis=2))
    outsides = (outside_first, outside_second, outside_third)
    layer_index = lax.broadcasted_iota(jnp.int32, (1, 1, layers, 1, 1, 1), 2)
    summed = jnp.zeros_like(nodal)
    for d, node_axis in enumerate((-3, -2, -1)):
        low_term = face_term(lower_side[d], outsides[d][0], lows[d], metric[..., d])
        high_term = face_term(upper_side[d], outsides[d][1], highs[d], metric[..., d])
        if d == 2:
            factor = 3.0 * metric[..., 2][..., None, None, None]
            low_term = jnp.where(layer_index == middle, factor * mortar_stator[:, :, None], low_term)
            high_term = jnp.where(layer_index == middle - 1, factor * mortar_rotor[:, :, None], high_term)
        summed = summed + place_faces(low_term, high_term, node_axis)
    return summed

def mortar_terms(rotor_slot, stator_slot, slot_tables, in_use, lower_side, upper_side):
    on_rotor = jnp.einsum('smi,srfij->srfmj', slot_tables[0], rotor_slot, precision=highest)
    on_stator = jnp.einsum('smi,srfij->srfmj', slot_tables[1], stator_slot, precision=highest)
    jump = on_rotor - on_stator
    weight = in_use[:, None, None, None, None]
    to_stator = jnp.einsum('sim,fg,srgmj->srfij', slot_tables[3], lower_side[2], jump, precision=highest) * weight
    to_rotor = jnp.einsum('sim,fg,srgmj->srfij', slot_tables[2], upper_side[2], -jump, precision=highest) * weight
    return (to_stator, to_rotor)

def tendency(solution, metric, intersections, counts, projections):
    derivative = derivative_table()
    jacobians, lower_side, upper_side = flux_tables()
    leading = solution.shape[:3]
    nodal = solution.reshape(leading + (5, 4, 4, 4))
    lows, highs = inside_traces(nodal)
    outside_first = (jnp.roll(highs[0], 1, axis=0), jnp.roll(lows[0], -1, axis=0))
    zero_row = jnp.zeros_like(highs[1][:, :1])
    outside_second = (jnp.concatenate([zero_row, highs[1][:, :-1]], axis=1), jnp.concatenate([lows[1][:, 1:], zero_row], axis=1))
    middle = leading[2] // 2
    rotor_faces = highs[2][:, :, middle - 1]
    stator_faces = lows[2][:, :, middle]
    sector = jnp.arange(N_AZIM, dtype=jnp.int32)
    home_sector = jnp.stack([(sector + N_AZIM - 1) % N_AZIM, sector], axis=1)
    rotor_index = (home_sector[:, :, None] * EA + intersections[:, :, 0, :]).reshape(-1)
    stator_index = (sector[:, None, None] * EA + intersections[:, :, 1, :]).reshape(-1)
    segment_kind = intersections[:, :, 2, :].reshape(-1)
    capacity = intersections.shape[-1]
    in_use = (jnp.arange(capacity, dtype=jnp.int32)[None, None, :] < counts[:, :, None]).astype(jnp.float32).reshape(-1)
    slot_tables = projections[:, segment_kind]
    to_stator, to_rotor = mortar_terms(rotor_faces[rotor_index], stator_faces[stator_index], slot_tables, in_use, lower_side, upper_side)
    mortar_stator = jnp.zeros_like(stator_faces).at[stator_index].add(to_stator)
    mortar_rotor = jnp.zeros_like(rotor_faces).at[rotor_index].add(to_rotor)
    blocks = lax.map(lambda pieces: volume_term(pieces[0], pieces[1], derivative, jacobians), (solution.reshape((N_AZIM, EA) + solution.shape[1:]), metric.reshape((N_AZIM, EA) + metric.shape[1:])))
    volume = blocks.reshape(solution.shape)
    faces = surface(nodal, metric, lows, highs, outside_first, outside_second, mortar_stator, mortar_rotor, lower_side, upper_side)
    return volume + faces.reshape(solution.shape)

def reference(solution, metric, intersections, counts, projections):
    section_one = solution + time_step * tendency(solution, metric, intersections, counts, projections)
    section_two = section_one + time_step * tendency(section_one, metric, intersections, counts, projections)
    return 0.5 * solution + 0.5 * section_two
```

```python
import functools
import jax
import jax.numpy as jnp
import numpy as np
from jax import lax
from jax.experimental import pallas as pl
from jax.experimental.pallas import tpu as pltpu
from jax.sharding import PartitionSpec as P

time_step = 0.02
mean_flow = (0.5, 0.0, 0.4)
speeds = tuple(abs(u) + 1.0 for u in mean_flow)
highest = lax.Precision.HIGHEST
f32 = jnp.float32


def line_numbers():
    points = np.array([-1.0, -1.0 / np.sqrt(5.0), 1.0 / np.sqrt(5.0), 1.0])
    barycentric = np.array(
        [1.0 / np.prod([points[j] - points[k] for k in range(4) if k != j]) for j in range(4)]
    )
    single = np.zeros((4, 4))
    for i in range(4):
        for j in range(4):
            if i != j:
                single[i, j] = barycentric[j] / barycentric[i] / (points[i] - points[j])
        single[i, i] = -np.sum(single[i])
    return single


D = line_numbers()


def row(f, i, j, k):
    return (f * 64 + 16 * i + 4 * j + k) * 8


def tile(ref, f, i, j, k):
    return ref[pl.ds(row(f, i, j, k), 8), :]


def lane_ids():
    return lax.broadcasted_iota(jnp.int32, (8, 128), 1)


def minus_slope(x, scale):
    e0, e1 = x[0] - x[3], x[1] - x[2]
    t = (x[0] + x[3]) - (x[1] + x[2])
    c = -scale * 0.5
    outer = (c * (D[0, 0] - D[0, 3])) * e0 + (c * (D[0, 1] - D[0, 2])) * e1
    inner = (c * (D[1, 0] - D[1, 3])) * e0 + (c * (D[1, 1] - D[1, 2])) * e1
    outer_t = (c * (D[0, 0] + D[0, 3])) * t
    inner_t = (c * (D[1, 0] + D[1, 3])) * t
    return [outer + outer_t, inner + inner_t, inner - inner_t, outer - outer_t]


def line_terms(d, x, low, high):
    flow, speed = mean_flow[d], speeds[d]
    w0 = [3.0 * v for v in low]
    w3 = [3.0 * v for v in high]
    mine = 1 + d
    slopes = {}
    for f in (mine, 4):
        h = minus_slope(x[f], 1.0)
        h[0] = h[0] + w0[f]
        h[3] = h[3] - w3[f]
        slopes[f] = h
    result = []
    for f in range(5):
        if f == mine:
            r = [slopes[4][i] + flow * slopes[mine][i] if flow else slopes[4][i] for i in range(4)]
            r[0] = r[0] + speed * w0[f]
            r[3] = r[3] + speed * w3[f]
        elif f == 4:
            r = [slopes[mine][i] + flow * slopes[4][i] if flow else slopes[mine][i] for i in range(4)]
            r[0] = r[0] + speed * w0[f]
            r[3] = r[3] + speed * w3[f]
        else:
            r = minus_slope(x[f], flow) if flow else [None] * 4
            if f == 0:
                r = [slopes[mine][i] if r[i] is None else r[i] + slopes[mine][i] for i in range(4)]
            lows, highs = (speed + flow) * w0[f], (speed - flow) * w3[f]
            r[0] = lows if r[0] is None else r[0] + lows
            r[3] = highs if r[3] is None else r[3] + highs
        result.append(r)
    return result


def apply_operator(q, m, acc, az, rad, mortar, first, write):
    lanes = lane_ids()
    axial = lanes & 15
    scale = m[pl.ds(16, 8), :]
    for i in range(4):
        for j in range(4):
            x = [[tile(q, f, i, j, k) for k in range(4)] for f in range(5)]
            low, high = [], []
            for f in range(5):
                before = jnp.where(axial == 0, 0.0, pltpu.roll(x[f][3], 1, 1))
                after = jnp.where(axial == 15, 0.0, pltpu.roll(x[f][0], 127, 1))
                to_stator, to_rotor = mortar(f, i, j)
                low.append(jnp.where(axial == 8, to_stator, before - x[f][0]))
                high.append(jnp.where(axial == 7, to_rotor, after - x[f][3]))
            terms = line_terms(2, x, low, high)
            for f in range(5):
                for k in range(4):
                    acc[pl.ds(row(f, i, j, k), 8), :] = first(x[f][k], f, i, j, k) + scale * terms[f][k]
    scale = m[pl.ds(0, 8), :]
    for j in range(4):
        for k in range(4):
            x = [[tile(q, f, i, j, k) for i in range(4)] for f in range(5)]
            low, high = [], []
            for f in range(5):
                before, after = az(f, j, k, x[f][0], x[f][3])
                low.append(before - x[f][0])
                high.append(after - x[f][3])
            terms = line_terms(0, x, low, high)
            for f in range(5):
                for i in range(4):
                    if terms[f][i] is not None:
                        at = pl.ds(row(f, i, j, k), 8)
                        acc[at, :] = acc[at, :] + scale * terms[f][i]
    scale = m[pl.ds(8, 8), :]
    for i in range(4):
        for k in range(4):
            x = [[tile(q, f, i, j, k) for j in range(4)] for f in range(5)]
            low, high = [], []
            for f in range(5):
                before, after = rad(f, i, k, x[f][0], x[f][3])
                low.append(before - x[f][0])
                high.append(after - x[f][3])
            terms = line_terms(1, x, low, high)
            for f in range(5):
                for j in range(4):
                    if terms[f][j] is not None:
                        at = pl.ds(row(f, i, j, k), 8)
                        write(f, i, j, k, acc[at, :] + scale * terms[f][j])
                    else:
                        write(f, i, j, k, None)


def pack_faces(q, par, own, az0, az1, r0, r1, lists):
    lanes = lane_ids()
    even = par[0] == 0
    for f in range(5):
        at = pl.ds(f * 16, 16)
        high = q[pl.ds((f * 64 + 48) * 8 + 7, 16, stride=8), :]
        low = q[pl.ds(f * 64 * 8, 16, stride=8), :]
        az0[at, :] = jnp.where(even, high, low)
        az1[at, :] = jnp.where(even, low, high)
    spot = lanes & 15
    for i in range(4):
        for block, fields in ((0, range(4)), (1, (4,))):
            rotor = jnp.zeros((8, 128), f32)
            stator = jnp.zeros((8, 128), f32)
            for f in fields:
                for j in range(4):
                    p = 4 * (f % 4) + j
                    rotor = jnp.where(spot == p, pltpu.roll(tile(q, f, i, j, 3), (p - 7) % 128, 1), rotor)
                    stator = jnp.where(spot == p, pltpu.roll(tile(q, f, i, j, 0), (p - 8) % 128, 1), stator)
            at = pl.ds(80 + block * 32 + i * 8, 8)
            az0[at, :] = jnp.where(even, rotor, stator)
            az1[at, :] = jnp.where(even, stator, rotor)
            own[pl.ds(block * 32 + i * 8, 8), :] = rotor
            own[pl.ds(64 + block * 32 + i * 8, 8), :] = stator
    if lists is not None:
        az0[pl.ds(144, 8), :] = lists[pl.ds(0, 8), :]
        az1[pl.ds(144, 8), :] = lists[pl.ds(0, 8), :]
    outward = par[1] == 0
    place = lanes >> 4
    for g in range(10):
        high = jnp.zeros((8, 128), f32)
        low = jnp.zeros((8, 128), f32)
        for p in range(8):
            f, n = divmod(g * 8 + p, 16)
            i, k = divmod(n, 4)
            high = jnp.where(place == p, pltpu.roll(tile(q, f, i, 3, k), (16 * (p - 7)) % 128, 1), high)
            low = jnp.where(place == p, pltpu.roll(tile(q, f, i, 0, k), (16 * p) % 128, 1), low)
        at = pl.ds(g * 8, 8)
        r0[at, :] = jnp.where(outward, high, low)
        r1[at, :] = jnp.where(outward, low, high)


def outsides(par, ga0, ga1, gr0, gr1):
    even = par[0] == 0
    outward = par[1] == 0
    sub = lax.broadcasted_iota(jnp.int32, (8, 128), 0)
    lanes = lane_ids()
    first, last = par[2] == 0, par[2] == 7

    def az(f, j, k, low_inside, high_inside):
        at = pl.ds(f * 16 + 4 * j + k, 1)
        one, two = ga0[at, :], ga1[at, :]
        before = jnp.where(even, two, one)
        after = jnp.where(even, one, two)
        return (
            jnp.where(sub == 0, before, pltpu.roll(high_inside, 1, 0)),
            jnp.where(sub == 7, after, pltpu.roll(low_inside, 7, 0)),
        )

    def rad(f, i, k, low_inside, high_inside):
        g, p = divmod(f * 16 + 4 * i + k, 8)
        at = pl.ds(g * 8, 8)
        one, two = gr0[at, :], gr1[at, :]
        before = jnp.where(first, 0.0, jnp.where(outward, two, one))
        after = jnp.where(last, 0.0, jnp.where(outward, one, two))
        high = jnp.where(lanes >= 112, pltpu.roll(before, (112 - 16 * p) % 128, 1), high_inside)
        low = jnp.where(lanes < 16, pltpu.roll(after, (128 - 16 * p) % 128, 1), low_inside)
        return pltpu.roll(high, 16, 1), pltpu.roll(low, 112, 1)

    return az, rad


def mortar_matrix(lists, following, tables):
    slots = jnp.concatenate([lists, following], axis=0)
    rotor, stator, kind, used = (slots[:, c : c + 1] for c in range(4))
    lanes = lax.broadcasted_iota(jnp.int32, (24, 128), 1)
    pick = (lanes.astype(f32) == kind).astype(f32)
    face = (lanes & 7).astype(f32)
    on_rotor = (face == rotor).astype(f32)
    on_stator = (face == stator).astype(f32) * 1.0
    entries = jnp.dot(pick, tables, precision=highest, preferred_element_type=f32)
    order = lax.broadcasted_iota(jnp.int32, (24, 128), 0)
    p_rot = entries[:, 0:128] * on_rotor
    p_sta = -entries[:, 128:256] * on_stator
    q_rot = -entries[:, 256:384] * on_rotor * used
    q_sta = entries[:, 384:512] * on_stator * used
    first = (order < 8).astype(f32)
    third = (order >= 16).astype(f32)
    b_parts = [p_rot * first, p_rot * (1.0 - first), p_sta * (1.0 - third), p_sta * third]
    c_parts = [q_sta * (1.0 - third), q_rot * (1.0 - first)]
    b_all = jnp.concatenate(
        [jnp.concatenate([b[:, 32 * m : 32 * m + 32] for b in b_parts], axis=1) for m in range(4)], axis=0
    )
    c_all = jnp.concatenate(
        [jnp.concatenate([c[:, 32 * m : 32 * m + 32] for c in c_parts], axis=1) for m in range(4)], axis=0
    )
    return lax.dot_general(
        c_all, b_all, (((0,), (0,)), ((), ())), precision=highest, preferred_element_type=f32
    )


def mortar_terms(par, matrix, own, ga0, ga1, placed):
    even = par[0] == 0
    blocks = []
    for block in range(2):
        at = pl.ds(80 + block * 32, 32)
        one, two = ga0[at, :], ga1[at, :]
        blocks.append(
            jnp.concatenate(
                [
                    jnp.where(even, two, one),
                    own[pl.ds(block * 32, 32), :],
                    own[pl.ds(64 + block * 32, 32), :],
                    jnp.where(even, one, two),
                ],
                axis=0,
            )
        )
    traces = jnp.concatenate(blocks, axis=1)
    placed[...] = jnp.dot(matrix, traces, precision=highest, preferred_element_type=f32)

    def mortar(f, i, j):
        block, p = divmod(4 * f + j, 16)
        at = pl.ds(128 * block, 128)
        to_stator = pltpu.roll(placed[pl.ds(8 * i, 8), at], (8 - p) % 128, 1)
        to_rotor = pltpu.roll(placed[pl.ds(32 + 8 * i, 8), at], (7 - p) % 128, 1)
        return to_stator, to_rotor

    return mortar


def enter_kernel(par, nat, metric, lists, q, m, own, az0, az1, r0, r1):
    for a in range(8):
        for c in (0, 128, 256):
            width = min(128, 320 - c)
            q[pl.ds(c * 8 + a, width, stride=8), :] = nat[a, :, c : c + width].T
        scaled = time_step * metric[a].T
        for d in range(3):
            m[pl.ds(d * 8 + a, 1), :] = scaled[d : d + 1]
    pack_faces(q, par, own, az0, az1, r0, r1, lists)


def middle_kernel(par, q, m, own, lists, tables, ga0, ga1, gr0, gr1, s, matrix, own2, az0, az1, r0, r1, placed):
    matrix[...] = mortar_matrix(lists[...], ga_lists(par, ga0, ga1), tables[...])
    mortar = mortar_terms(par, matrix[...], own, ga0, ga1, placed)
    az, rad = outsides(par, ga0, ga1, gr0, gr1)

    def write(f, i, j, k, value):
        if value is not None:
            s[pl.ds(row(f, i, j, k), 8), :] = value

    apply_operator(q, m, s, az, rad, mortar, lambda x, *at: x, write)
    pack_faces(s, par, own2, az0, az1, r0, r1, None)


def ga_lists(par, ga0, ga1):
    return jnp.where(par[0] == 0, ga0[pl.ds(144, 8), :], ga1[pl.ds(144, 8), :])


def last_kernel(par, q, s, m, own, matrix, ga0, ga1, gr0, gr1, out, acc, placed):
    mortar = mortar_terms(par, matrix[...], own, ga0, ga1, placed)
    az, rad = outsides(par, ga0, ga1, gr0, gr1)

    def write(f, i, j, k, value):
        at = pl.ds(row(f, i, j, k), 8)
        acc[at, :] = 0.5 * ((acc[at, :] if value is None else value) + q[at, :])

    apply_operator(s, m, acc, az, rad, mortar, lambda x, *at: x, write)
    for a in range(8):
        for c in (0, 128, 256):
            width = min(128, 320 - c)
            out[a, :, c : c + width] = acc[pl.ds(c * 8 + a, width, stride=8), :].T


def call(kernel, outs, scratch=()):
    vmem = pl.BlockSpec(memory_space=pltpu.VMEM)
    smem = pl.BlockSpec(memory_space=pltpu.SMEM)

    def run(par, *args):
        return pl.pallas_call(
            kernel,
            out_shape=[jax.ShapeDtypeStruct(s, f32) for s in outs],
            in_specs=[smem] + [vmem] * len(args),
            out_specs=[vmem] * len(outs),
            scratch_shapes=[pltpu.VMEM(s, f32) for s in scratch],
            compiler_params=pltpu.CompilerParams(vmem_limit_bytes=32 * 2**20),
        )(par, *args)

    return run


def exchange(az0, az1, r0, r1, sectors, blocks):
    both = ("azim", "radax")
    at = lambda a, r: (a % sectors) * blocks + r
    on0 = [(a, a ^ 1) for a in range(sectors)]
    on1 = [(a, (a + 1 if a % 2 else a - 1) % sectors) for a in range(sectors)]
    rad0 = [(r, r ^ 1) for r in range(blocks)]
    rad1 = []
    for a in range(sectors):
        for r in range(blocks):
            if r in (0, blocks - 1):
                rad1.append((at(a, r), at(a ^ 1, r)))
            else:
                rad1.append((at(a, r), at(a, r + 1 if r % 2 else r - 1)))
    g1 = lax.ppermute(r1, both, rad1)
    ga1 = lax.ppermute(az1, "azim", on1)
    g0 = lax.ppermute(r0, "radax", rad0)
    ga0 = lax.ppermute(az0, "azim", on0)
    return ga0, ga1, g0, g1


def shards(solution, metric, intersections, counts, projections):
    sectors, blocks = lax.axis_size("azim"), lax.axis_size("radax")
    azim, radax = lax.axis_index("azim"), lax.axis_index("radax")
    par = jnp.stack([azim % 2, radax % 2, radax, azim]).astype(jnp.int32)
    in_use = lax.broadcasted_iota(jnp.int32, (2, 8), 1) < counts[0][:, None]
    lists = jnp.concatenate([intersections[0], in_use[:, None].astype(jnp.int32)], axis=1)
    lists = lists.transpose(0, 2, 1).reshape(16, 4).astype(f32)
    lists = jnp.pad(lists, ((0, 0), (0, 124)))
    turned = jnp.concatenate([projections[:2], projections[2:].transpose(0, 1, 3, 2)], axis=0)
    tables = jnp.repeat(turned.transpose(1, 0, 2, 3).reshape(16, 64), 8, axis=1)
    tables = jnp.pad(tables, ((0, 112), (0, 0)))
    nat = solution.reshape(8, 128, 320)
    state = (2560, 128)
    faces = [(152, 128), (152, 128), (80, 128), (80, 128)]
    small = [(144, 128), (144, 128), (80, 128), (80, 128)]
    q, m, own, *sent = call(enter_kernel, [state, (24, 128), (128, 128)] + faces)(
        par, nat, metric.reshape(8, 128, 3), lists
    )
    got = exchange(*sent, sectors, blocks)
    s, matrix, own2, *sent = call(
        middle_kernel, [state, (64, 128), (128, 128)] + small, [(64, 256)]
    )(par, q, m, own, lists, tables, *got)
    got = exchange(*sent, sectors, blocks)
    (out,) = call(last_kernel, [(8, 128, 320)], [state, (64, 256)])(par, q, s, m, own2, matrix, *got)
    return out.reshape(solution.shape)


def solution(mesh):
    in_specs = (
        P("azim", "radax", None, None),
        P("azim", "radax", None, None),
        P("azim", None, None, None),
        P("azim", None),
        P(),
    )
    out_specs = P("azim", "radax", None, None)
    return jax.shard_map(shards, mesh=mesh, in_specs=in_specs, out_specs=out_specs, check_vma=False)
```

```python
import functools
import jax
import jax.numpy as jnp
import numpy as np
from jax import lax
from jax.experimental import pallas as pl
from jax.experimental.pallas import tpu as pltpu
from jax.sharding import PartitionSpec as P

time_step = 0.02
mean_flow = (0.5, 0.0, 0.4)
speeds = tuple(abs(u) + 1.0 for u in mean_flow)
highest = lax.Precision.HIGHEST
f32 = jnp.float32


def line_numbers():
    points = np.array([-1.0, -1.0 / np.sqrt(5.0), 1.0 / np.sqrt(5.0), 1.0])
    barycentric = np.array(
        [1.0 / np.prod([points[j] - points[k] for k in range(4) if k != j]) for j in range(4)]
    )
    single = np.zeros((4, 4))
    for i in range(4):
        for j in range(4):
            if i != j:
                single[i, j] = barycentric[j] / barycentric[i] / (points[i] - points[j])
        single[i, i] = -np.sum(single[i])
    return single


D = line_numbers()


def row(f, i, j, k):
    return (f * 64 + 16 * i + 4 * j + k) * 8


def tile(ref, f, i, j, k):
    return ref[pl.ds(row(f, i, j, k), 8), :]


def lane_ids():
    return lax.broadcasted_iota(jnp.int32, (8, 128), 1)


def minus_slope(x, scale):
    e0, e1 = x[0] - x[3], x[1] - x[2]
    t = (x[0] + x[3]) - (x[1] + x[2])
    c = -scale * 0.5
    outer = (c * (D[0, 0] - D[0, 3])) * e0 + (c * (D[0, 1] - D[0, 2])) * e1
    inner = (c * (D[1, 0] - D[1, 3])) * e0 + (c * (D[1, 1] - D[1, 2])) * e1
    outer_t = (c * (D[0, 0] + D[0, 3])) * t
    inner_t = (c * (D[1, 0] + D[1, 3])) * t
    return [outer + outer_t, inner + inner_t, inner - inner_t, outer - outer_t]


def line_terms(d, x, low, high):
    flow, speed = mean_flow[d], speeds[d]
    w0 = [3.0 * v for v in low]
    w3 = [3.0 * v for v in high]
    mine = 1 + d
    slopes = {}
    for f in (mine, 4):
        h = minus_slope(x[f], 1.0)
        h[0] = h[0] + w0[f]
        h[3] = h[3] - w3[f]
        slopes[f] = h
    result = []
    for f in range(5):
        if f == mine:
            r = [slopes[4][i] + flow * slopes[mine][i] if flow else slopes[4][i] for i in range(4)]
            r[0] = r[0] + speed * w0[f]
            r[3] = r[3] + speed * w3[f]
        elif f == 4:
            r = [slopes[mine][i] + flow * slopes[4][i] if flow else slopes[mine][i] for i in range(4)]
            r[0] = r[0] + speed * w0[f]
            r[3] = r[3] + speed * w3[f]
        else:
            r = minus_slope(x[f], flow) if flow else [None] * 4
            if f == 0:
                r = [slopes[mine][i] if r[i] is None else r[i] + slopes[mine][i] for i in range(4)]
            lows, highs = (speed + flow) * w0[f], (speed - flow) * w3[f]
            r[0] = lows if r[0] is None else r[0] + lows
            r[3] = highs if r[3] is None else r[3] + highs
        result.append(r)
    return result


def position():
    azim, radax = lax.axis_index("azim"), lax.axis_index("radax")
    return azim & 1, radax & 1, radax


def staged(lines, fetch, finish):
    ready = fetch(*lines[0])
    for at, line in enumerate(lines):
        later = fetch(*lines[at + 1]) if at + 1 < len(lines) else None
        finish(*line, *ready)
        ready = later


def pairs():
    return [(p, r) for p in range(4) for r in range(4)]


def inner_operator(q, m, acc, first):
    lanes = lane_ids()
    sub = lax.broadcasted_iota(jnp.int32, (8, 128), 0)
    axial = lanes & 15

    def passes(d, nodes, low_of, high_of, put):
        scale = m[pl.ds(8 * d, 8), :]

        def fetch(p, r):
            low, high = [], []
            for f in range(5):
                x0, x3 = tile(q, f, *nodes(p, r, 0)), tile(q, f, *nodes(p, r, 3))
                low.append(low_of(x0, x3))
                high.append(high_of(x0, x3))
            return low, high

        def finish(p, r, low, high):
            x = [[tile(q, f, *nodes(p, r, e)) for e in range(4)] for f in range(5)]
            terms = line_terms(d, x, low, high)
            for f in range(5):
                for e in range(4):
                    if terms[f][e] is not None:
                        put(f, *nodes(p, r, e), x[f][e], scale * terms[f][e])

        staged(pairs(), fetch, finish)

    def begin(f, i, j, k, x, term):
        acc[pl.ds(row(f, i, j, k), 8), :] = first(x, f, i, j, k) + term

    def add(f, i, j, k, x, term):
        at = pl.ds(row(f, i, j, k), 8)
        acc[at, :] = acc[at, :] + term

    def axial_low(x0, x3):
        outside = jnp.where(axial == 0, 0.0, pltpu.roll(x3, 1, 1))
        return jnp.where(axial == 8, 0.0, outside - x0)

    def axial_high(x0, x3):
        outside = jnp.where(axial == 15, 0.0, pltpu.roll(x0, 127, 1))
        return jnp.where(axial == 7, 0.0, outside - x3)

    passes(2, lambda i, j, k: (i, j, k), axial_low, axial_high, begin)
    passes(
        0,
        lambda j, k, i: (i, j, k),
        lambda x0, x3: jnp.where(sub == 0, 0.0, pltpu.roll(x3, 1, 0) - x0),
        lambda x0, x3: jnp.where(sub == 7, 0.0, pltpu.roll(x0, 7, 0) - x3),
        add,
    )
    passes(
        1,
        lambda i, k, j: (i, j, k),
        lambda x0, x3: jnp.where(lanes < 16, 0.0, pltpu.roll(x3, 16, 1) - x0),
        lambda x0, x3: jnp.where(lanes >= 112, 0.0, pltpu.roll(x0, 112, 1) - x3),
        add,
    )


def coupled(f, d):
    return 4 if f == 1 + d else 1 + d if f in (0, 4) else None


def end_terms(q, m, base, acc, factor, fields, sides):
    for f in fields:
        for i, j in pairs():
            at = pl.ds(row(f, i, j, 1), 16)
            acc[at, :] = base[at, :]
    for d, nodes in (
        (2, lambda i, j, k: (i, j, k)),
        (0, lambda j, k, i: (i, j, k)),
        (1, lambda i, k, j: (i, j, k)),
    ):
        scale = (3.0 * factor) * m[pl.ds(8 * d, 8), :]
        flow, speed = mean_flow[d], speeds[d]
        old = base if d == 2 else acc
        needed = sorted(set(fields) | {coupled(f, d) for f in fields} - {None})

        def fetch(p, r):
            return ({f: sides[d](f, p, r, tile(q, f, *nodes(p, r, 0)), tile(q, f, *nodes(p, r, 3))) for f in needed},)

        def finish(p, r, jumps):
            for f in fields:
                other = coupled(f, d)
                for end, sign in ((0, 1.0), (1, -1.0)):
                    term = (speed + sign * flow) * jumps[f][end]
                    if other is not None:
                        term = term + jumps[other][end] if end == 0 else term - jumps[other][end]
                    at = pl.ds(row(f, *nodes(p, r, 3 * end)), 8)
                    acc[at, :] = old[at, :] + scale * term

        staged(pairs(), fetch, finish)


def pack_sector(q, side, message):
    spot = (lane_ids() + side) & 15
    for f in range(5):
        low = q[pl.ds(f * 64 * 8, 16, stride=8), :]
        high = q[pl.ds((f * 64 + 48) * 8 + 7, 16, stride=8), :]
        message[pl.ds(f * 16, 16), :] = jnp.where(side == 0, low, high)
    for i in range(4):
        for block, fields in ((0, range(4)), (1, (4,))):
            packed = jnp.zeros((8, 128), f32)
            for f in fields:
                for j in range(4):
                    p = 4 * (f % 4) + j
                    at = pl.multiple_of(row(f, i, j, 0) + 24 * side, 8)
                    packed = jnp.where(spot == p, pltpu.roll(q[pl.ds(at, 8), :], (120 + p) % 128, 1), packed)
            message[pl.ds(80 + block * 32 + i * 8, 8), :] = pltpu.roll(packed, side, 1)


def pack_blocks(q, side, message):
    place = ((lane_ids() >> 4) + side) & 7
    for g in range(10):
        packed = jnp.zeros((8, 128), f32)
        for p in range(8):
            f, n = divmod(g * 8 + p, 16)
            i, k = divmod(n, 4)
            at = pl.multiple_of(row(f, i, 0, k) + 96 * side, 8)
            packed = jnp.where(place == p, pltpu.roll(q[pl.ds(at, 8), :], 16 * p, 1), packed)
        message[pl.ds(g * 8, 8), :] = pltpu.roll(packed, 16 * side, 1)


def choose(par, ga0, ga1, gr0, gr1, back, ahead, below, above):
    even = par[0] == 0
    outward = par[1] == 0
    rows = back.shape[0]
    one, two = ga0[pl.ds(0, rows), :], ga1[pl.ds(0, rows), :]
    back[...] = jnp.where(even, two, one)
    ahead[...] = jnp.where(even, one, two)
    one, two = gr0[pl.ds(0, 80), :], gr1[pl.ds(0, 80), :]
    below[...] = jnp.where(par[2] == 0, 0.0, jnp.where(outward, two, one))
    above[...] = jnp.where(par[2] == 7, 0.0, jnp.where(outward, one, two))


def outside_jumps(back, ahead, below, above, by_rows, mortar):
    sub = lax.broadcasted_iota(jnp.int32, (8, 128), 0)
    lanes = lane_ids()
    axial = lanes & 15

    def az(f, j, k, x0, x3):
        at = pl.ds(f * 16 + 4 * j + k, 1)
        return jnp.where(sub == 0, back[at, :] - x0, 0.0), jnp.where(sub == 7, ahead[at, :] - x3, 0.0)

    def rad(f, i, k, x0, x3):
        n = f * 16 + 4 * i + k
        if by_rows:
            at = pl.ds(n, 1)
            before = pltpu.roll(jnp.broadcast_to(below[at, :], (8, 128)), 16, 1, stride=16, stride_axis=0)
            after = pltpu.roll(jnp.broadcast_to(above[at, :], (8, 128)), 0, 1, stride=16, stride_axis=0)
        else:
            g, p = divmod(n, 8)
            at = pl.ds(g * 8, 8)
            before = pltpu.roll(below[at, :], (128 - 16 * p) % 128, 1)
            after = pltpu.roll(above[at, :], (112 - 16 * p) % 128, 1)
        return jnp.where(lanes < 16, before - x0, 0.0), jnp.where(lanes >= 112, after - x3, 0.0)

    def ax(f, i, j, x0, x3):
        to_stator, to_rotor = mortar(f, i, j)
        return jnp.where(axial == 8, to_stator, 0.0), jnp.where(axial == 7, to_rotor, 0.0)

    return {0: az, 1: rad, 2: ax}


def mortar_matrix(lists, following, tables):
    own, later = lists.T, following.T

    def column(t):
        return jnp.concatenate([own[0:8, t : t + 1], own[0:8, t + 3 : t + 4], later[0:8, t : t + 1]], axis=0)

    rotor, stator, kind = (column(t) for t in range(3))
    slot = lax.broadcasted_iota(jnp.int32, (24, 1), 0)
    filled = jnp.concatenate(
        [
            jnp.broadcast_to(lists[6:7, 0:1], (8, 1)),
            jnp.broadcast_to(lists[7:8, 0:1], (8, 1)),
            jnp.broadcast_to(following[6:7, 0:1], (8, 1)),
        ],
        axis=0,
    )
    used = ((slot & 7).astype(f32) < filled).astype(f32)
    lanes = lax.broadcasted_iota(jnp.int32, (24, 128), 1)
    pick = (lanes.astype(f32) == kind).astype(f32)
    face = (lanes & 7).astype(f32)
    on_rotor = (face == rotor).astype(f32)
    on_stator = (face == stator).astype(f32) * 1.0
    entries = jnp.dot(pick, tables, precision=highest, preferred_element_type=f32)
    order = lax.broadcasted_iota(jnp.int32, (24, 128), 0)
    p_rot = entries[:, 0:128] * on_rotor
    p_sta = -entries[:, 128:256] * on_stator
    q_rot = -entries[:, 256:384] * on_rotor * used
    q_sta = entries[:, 384:512] * on_stator * used
    first = (order < 8).astype(f32)
    third = (order >= 16).astype(f32)
    b_parts = [p_rot * first, p_rot * (1.0 - first), p_sta * (1.0 - third), p_sta * third]
    c_parts = [q_sta * (1.0 - third), q_rot * (1.0 - first)]
    b_all = jnp.concatenate(
        [jnp.concatenate([b[:, 32 * m : 32 * m + 32] for b in b_parts], axis=1) for m in range(4)], axis=0
    )
    c_all = jnp.concatenate(
        [jnp.concatenate([c[:, 32 * m : 32 * m + 32] for c in c_parts], axis=1) for m in range(4)], axis=0
    )
    return lax.dot_general(
        c_all, b_all, (((0,), (0,)), ((), ())), precision=highest, preferred_element_type=f32
    )


def mortar_terms(par, matrix, s0, s1, back, ahead, placed):
    even = par[0] == 0
    blocks = []
    for block in range(2):
        at = pl.ds(80 + block * 32, 32)
        one, two = s0[at, :], s1[at, :]
        mine, yours = jnp.where(even, one, two), jnp.where(even, two, one)
        blocks.append(jnp.concatenate([back[at, :], mine, yours, ahead[at, :]], axis=0))
    traces = jnp.concatenate(blocks, axis=1)
    placed[...] = jnp.dot(matrix, traces, precision=highest, preferred_element_type=f32)

    def mortar(f, i, j):
        block, p = divmod(4 * f + j, 16)
        at = pl.ds(128 * block, 128)
        to_stator = pltpu.roll(placed[pl.ds(8 * i, 8), at], (8 - p) % 128, 1)
        to_rotor = pltpu.roll(placed[pl.ds(32 + 8 * i, 8), at], (7 - p) % 128, 1)
        return to_stator, to_rotor

    return mortar


def rim_kernel(state, r0, r1, rims, sems):
    par = position()
    copies = [pltpu.make_async_copy(state.at[:, 7 * e], rims.at[e], sems.at[e]) for e in range(2)]
    for copy in copies:
        copy.start()
    for e in range(2):
        copies[e].wait()
    even = par[1] == 0
    for c in (0, 128, 256):
        width = min(128, 320 - c)
        low, high = (
            jnp.concatenate([rims[e, 7 - a, :, c : c + width] for a in range(8)], axis=0).T for e in range(2)
        )
        for g in range(width // 16):
            at = 16 * g
            down, up = low[at : at + 4], high[at + 12 : at + 16]
            r1[pl.ds(c // 4 + 4 * g, 4), :] = jnp.where(even, down, up)
            r0[pl.ds(c // 4 + 4 * g, 4), :] = jnp.where(even, up, down)


def enter_kernel(counts, nat, slots, q, s1):
    par = position()
    for a in range(8):
        for c in (0, 128, 256):
            width = min(128, 320 - c)
            q[pl.ds(c * 8 + a, width, stride=8), :] = nat[a, :, c : c + width].T
    pack_sector(q, par[0], s1)
    lists = jnp.concatenate(
        [
            jnp.concatenate([slots[b].astype(f32) for b in range(2)], axis=0),
            jnp.concatenate(
                [jnp.broadcast_to(counts[:, b : b + 1].astype(f32), (1, 8)) for b in range(2)], axis=0
            ),
        ],
        axis=0,
    )
    s1[pl.ds(144, 8), :] = jnp.concatenate([lists, jnp.zeros((8, 120), f32)], axis=1)


def others_kernel(q, s1, s0):
    par = position()
    pack_sector(q, 1 - par[0], s0)
    s0[pl.ds(144, 8), :] = s1[pl.ds(144, 8), :]


def inner_kernel(q, m, acc):
    inner_operator(q, m, acc, lambda x, *at: x)


def middle_kernel(
    inner, q, m, s0, s1, tables, ga0, ga1, gr0, gr1, s, matrix, r1, placed, back, ahead, below, above
):
    par = position()
    choose(par, ga0, ga1, gr0, gr1, back, ahead, below, above)
    matrix[...] = mortar_matrix(s1[pl.ds(144, 8), :], ahead[pl.ds(144, 8), :], tables[...])
    mortar = mortar_terms(par, matrix[...], s0, s1, back, ahead, placed)
    end_terms(q, m, inner, s, 1.0, range(5), outside_jumps(back, ahead, below, above, True, mortar))
    pack_blocks(s, par[1], r1)
    r1[pl.ds(80, 72), :] = jnp.zeros((72, 128), f32)


def sector_kernel(s, s1):
    par = position()
    pack_sector(s, par[0], s1)


def later_kernel(s, s0, r0):
    par = position()
    pack_blocks(s, 1 - par[1], r0)
    pack_sector(s, 1 - par[0], s0)


def inner_last_kernel(s, m, q, acc):
    half = {8 * d: 0.5 * m[pl.ds(8 * d, 8), :] for d in range(3)}

    class Halved:
        def __getitem__(self, at):
            return half[at[0].start]

    inner_operator(s, Halved(), acc, lambda x, *at: 0.5 * (x + tile(q, *at)))


def last_kernel(
    inner, s, m, s0, s1, matrix, ga0, ga1, gr0, gr1, out, acc, placed, back, ahead, below, above, turned, sems
):
    par = position()
    choose(par, ga0, ga1, gr0, gr1, back, ahead, below, above)
    mortar = mortar_terms(par, matrix[...], s0, s1, back, ahead, placed)
    jumps = outside_jumps(back, ahead, below, above, False, mortar)
    copies = []
    for c, fields in ((128, (2, 3)), (0, (0, 1)), (256, (4,))):
        width = min(128, 320 - c)
        end_terms(s, m, inner, acc, 0.5, fields, jumps)
        for a in range(8):
            turned[a, :, c : c + width] = acc[pl.ds(c * 8 + a, width, stride=8), :].T
            copies.append(
                pltpu.make_async_copy(
                    turned.at[a, :, pl.ds(c, width)], out.at[a, :, pl.ds(c, width)], sems.at[len(copies)]
                )
            )
            copies[-1].start()
    for copy in copies:
        copy.wait()


def call(kernel, outs, scratch=(), where={}, out_where=pltpu.VMEM, limit=32, cost=1):
    def run(*args):
        return pl.pallas_call(
            kernel,
            out_shape=[jax.ShapeDtypeStruct(s, f32) for s in outs],
            in_specs=[pl.BlockSpec(memory_space=where.get(n, pltpu.VMEM)) for n in range(len(args))],
            out_specs=[pl.BlockSpec(memory_space=out_where)] * len(outs),
            scratch_shapes=[s if not isinstance(s, tuple) else pltpu.VMEM(s, f32) for s in scratch],
            compiler_params=pltpu.CompilerParams(vmem_limit_bytes=limit * 2**20),
            cost_estimate=pl.CostEstimate(flops=0, transcendentals=0, bytes_accessed=cost * 3_000_000),
        )(*args)

    return run


def pairings(sectors, blocks):
    at = lambda a, r: (a % sectors) * blocks + r
    az0 = [(a, a ^ 1) for a in range(sectors)]
    az1 = [(a, (a + 1 if a % 2 else a - 1) % sectors) for a in range(sectors)]
    rad0 = [(r, r ^ 1) for r in range(blocks)]
    rad1 = []
    for a in range(sectors):
        for r in range(blocks):
            if r in (0, blocks - 1):
                rad1.append((at(a, r), at(a ^ 1, r)))
            else:
                rad1.append((at(a, r), at(a, r + 1 if r % 2 else r - 1)))
    return az0, az1, rad0, rad1


def shards(solution, metric, intersections, counts, projections):
    sectors, blocks = lax.axis_size("azim"), lax.axis_size("radax")
    az0, az1, rad0, rad1 = pairings(sectors, blocks)

    def across(r0, r1, s0, s1):
        gr1 = lax.ppermute(r1, ("azim", "radax"), rad1)
        gs1 = lax.ppermute(s1, "azim", az1)
        gr0 = lax.ppermute(r0, "radax", rad0)
        gs0 = lax.ppermute(s0, "azim", az0)
        return gs0, gs1, gr0, gr1

    state, rim, trace, first_trace = (2560, 128), (80, 128), (144, 128), (152, 128)
    dma = pltpu.SemaphoreType.DMA
    r0, r1 = call(rim_kernel, [rim, rim], [(2, 8, 16, 320), dma((2,))], {0: pltpu.HBM}, limit=53)(solution)
    turned = jnp.concatenate([projections[:2], projections[2:].transpose(0, 1, 3, 2)], axis=0)
    tables = jnp.repeat(turned.transpose(1, 0, 2, 3).reshape(16, 64), 8, axis=1)
    tables = jnp.pad(tables, ((0, 112), (0, 0)))
    m = time_step * metric.transpose(3, 0, 1, 2).reshape(24, 128)
    nat = solution.reshape(8, 128, 320)
    q, s1 = call(enter_kernel, [state, first_trace])(counts, nat, intersections[0])
    (s0,) = call(others_kernel, [first_trace])(q, s1)
    got = across(r0, r1, s0, s1)
    (inner,) = call(inner_kernel, [state])(q, m)
    sides = [(64, 256), first_trace, first_trace, rim, rim]
    s, matrix, r1 = call(middle_kernel, [state, (64, 128), first_trace], sides)(
        inner, q, m, s0, s1, tables, *got
    )
    (s1,) = call(sector_kernel, [trace])(s)
    s0, r0 = call(later_kernel, [trace, rim])(s)
    got = across(r0, r1, s0, s1)
    (inner,) = call(inner_last_kernel, [state])(s, m, q)
    sides = [state, (64, 256), trace, trace, rim, rim]
    (out,) = call(last_kernel, [(8, 128, 320)], sides + [(8, 128, 320), dma((24,))], {}, pltpu.HBM)(
        inner, s, m, s0, s1, matrix, *got
    )
    return out.reshape(solution.shape)


def solution(mesh):
    in_specs = (
        P("azim", "radax", None, None),
        P("azim", "radax", None, None),
        P("azim", None, None, None),
        P("azim", None),
        P(),
    )
    out_specs = P("azim", "radax", None, None)
    return jax.shard_map(shards, mesh=mesh, in_specs=in_specs, out_specs=out_specs, check_vma=False)
```

```python
import functools
import jax
import jax.numpy as jnp
import numpy as np
from jax import lax
from jax.experimental import pallas as pl
from jax.experimental.pallas import tpu as pltpu
from jax.sharding import PartitionSpec as P

time_step = 0.02
mean_flow = (0.5, 0.0, 0.4)
speeds = tuple(abs(u) + 1.0 for u in mean_flow)
highest = lax.Precision.HIGHEST
f32 = jnp.float32


def line_numbers():
    points = np.array([-1.0, -1.0 / np.sqrt(5.0), 1.0 / np.sqrt(5.0), 1.0])
    barycentric = np.array(
        [1.0 / np.prod([points[j] - points[k] for k in range(4) if k != j]) for j in range(4)]
    )
    single = np.zeros((4, 4))
    for i in range(4):
        for j in range(4):
            if i != j:
                single[i, j] = barycentric[j] / barycentric[i] / (points[i] - points[j])
        single[i, i] = -np.sum(single[i])
    return single


D = line_numbers()


def row(f, i, j, k):
    return (f * 64 + 16 * i + 4 * j + k) * 8


def tile(ref, f, i, j, k):
    return ref[pl.ds(row(f, i, j, k), 8), :]


def lane_ids():
    return lax.broadcasted_iota(jnp.int32, (8, 128), 1)


def minus_slope(x, scale):
    e0, e1 = x[0] - x[3], x[1] - x[2]
    t = (x[0] + x[3]) - (x[1] + x[2])
    c = -scale * 0.5
    outer = (c * (D[0, 0] - D[0, 3])) * e0 + (c * (D[0, 1] - D[0, 2])) * e1
    inner = (c * (D[1, 0] - D[1, 3])) * e0 + (c * (D[1, 1] - D[1, 2])) * e1
    outer_t = (c * (D[0, 0] + D[0, 3])) * t
    inner_t = (c * (D[1, 0] + D[1, 3])) * t
    return [outer + outer_t, inner + inner_t, inner - inner_t, outer - outer_t]


def line_terms(d, x, low, high):
    flow, speed = mean_flow[d], speeds[d]
    w0 = [3.0 * v for v in low]
    w3 = [3.0 * v for v in high]
    mine = 1 + d
    slopes = {}
    for f in (mine, 4):
        h = minus_slope(x[f], 1.0)
        h[0] = h[0] + w0[f]
        h[3] = h[3] - w3[f]
        slopes[f] = h
    result = []
    for f in range(5):
        if f == mine:
            r = [slopes[4][i] + flow * slopes[mine][i] if flow else slopes[4][i] for i in range(4)]
            r[0] = r[0] + speed * w0[f]
            r[3] = r[3] + speed * w3[f]
        elif f == 4:
            r = [slopes[mine][i] + flow * slopes[4][i] if flow else slopes[mine][i] for i in range(4)]
            r[0] = r[0] + speed * w0[f]
            r[3] = r[3] + speed * w3[f]
        else:
            r = minus_slope(x[f], flow) if flow else [None] * 4
            if f == 0:
                r = [slopes[mine][i] if r[i] is None else r[i] + slopes[mine][i] for i in range(4)]
            lows, highs = (speed + flow) * w0[f], (speed - flow) * w3[f]
            r[0] = lows if r[0] is None else r[0] + lows
            r[3] = highs if r[3] is None else r[3] + highs
        result.append(r)
    return result


def position():
    azim, radax = lax.axis_index("azim"), lax.axis_index("radax")
    return azim & 1, radax & 1, radax, azim


def staged(lines, fetch, finish):
    ready = fetch(*lines[0])
    for at, line in enumerate(lines):
        later = fetch(*lines[at + 1]) if at + 1 < len(lines) else None
        finish(*line, *ready)
        ready = later


def pairs():
    return [(p, r) for p in range(4) for r in range(4)]


def inner_operator(q, m, acc, first):
    lanes = lane_ids()
    sub = lax.broadcasted_iota(jnp.int32, (8, 128), 0)
    axial = lanes & 15

    def passes(d, nodes, low_of, high_of, put):
        scale = m[pl.ds(8 * d, 8), :]

        def fetch(p, r):
            low, high = [], []
            for f in range(5):
                x0, x3 = tile(q, f, *nodes(p, r, 0)), tile(q, f, *nodes(p, r, 3))
                low.append(low_of(x0, x3))
                high.append(high_of(x0, x3))
            return low, high

        def finish(p, r, low, high):
            x = [[tile(q, f, *nodes(p, r, e)) for e in range(4)] for f in range(5)]
            terms = line_terms(d, x, low, high)
            for f in range(5):
                for e in range(4):
                    if terms[f][e] is not None:
                        put(f, *nodes(p, r, e), x[f][e], scale * terms[f][e])

        staged(pairs(), fetch, finish)

    def begin(f, i, j, k, x, term):
        acc[pl.ds(row(f, i, j, k), 8), :] = first(x, f, i, j, k) + term

    def add(f, i, j, k, x, term):
        at = pl.ds(row(f, i, j, k), 8)
        acc[at, :] = acc[at, :] + term

    def axial_low(x0, x3):
        outside = jnp.where(axial == 0, 0.0, pltpu.roll(x3, 1, 1))
        return jnp.where(axial == 8, 0.0, outside - x0)

    def axial_high(x0, x3):
        outside = jnp.where(axial == 15, 0.0, pltpu.roll(x0, 127, 1))
        return jnp.where(axial == 7, 0.0, outside - x3)

    passes(2, lambda i, j, k: (i, j, k), axial_low, axial_high, begin)
    passes(
        0,
        lambda j, k, i: (i, j, k),
        lambda x0, x3: jnp.where(sub == 0, 0.0, pltpu.roll(x3, 1, 0) - x0),
        lambda x0, x3: jnp.where(sub == 7, 0.0, pltpu.roll(x0, 7, 0) - x3),
        add,
    )
    passes(
        1,
        lambda i, k, j: (i, j, k),
        lambda x0, x3: jnp.where(lanes < 16, 0.0, pltpu.roll(x3, 16, 1) - x0),
        lambda x0, x3: jnp.where(lanes >= 112, 0.0, pltpu.roll(x0, 112, 1) - x3),
        add,
    )


def coupled(f, d):
    return 4 if f == 1 + d else 1 + d if f in (0, 4) else None


def end_terms(q, m, base, acc, factor, fields, sides, directions=(2, 0, 1)):
    for f in fields:
        for i, j in pairs():
            at = pl.ds(row(f, i, j, 1), 16)
            acc[at, :] = base[at, :]
    for d in directions:
        nodes = (lambda j, k, i: (i, j, k), lambda i, k, j: (i, j, k), lambda i, j, k: (i, j, k))[d]
        scale = (3.0 * factor) * m[pl.ds(8 * d, 8), :]
        flow, speed = mean_flow[d], speeds[d]
        old = base if d == 2 else acc
        needed = sorted(set(fields) | {coupled(f, d) for f in fields} - {None})

        def fetch(p, r):
            return ({f: sides[d](f, p, r, tile(q, f, *nodes(p, r, 0)), tile(q, f, *nodes(p, r, 3))) for f in needed},)

        def finish(p, r, jumps):
            for f in fields:
                other = coupled(f, d)
                for end, sign in ((0, 1.0), (1, -1.0)):
                    term = (speed + sign * flow) * jumps[f][end]
                    if other is not None:
                        term = term + jumps[other][end] if end == 0 else term - jumps[other][end]
                    at = pl.ds(row(f, *nodes(p, r, 3 * end)), 8)
                    acc[at, :] = old[at, :] + scale * term

        staged(pairs(), fetch, finish)


def pack_sector(q, side, message):
    spot = (lane_ids() + side) & 15
    for f in range(5):
        low = q[pl.ds(f * 64 * 8, 16, stride=8), :]
        high = q[pl.ds((f * 64 + 48) * 8 + 7, 16, stride=8), :]
        message[pl.ds(f * 16, 16), :] = jnp.where(side == 0, low, high)
    for i in range(4):
        for block, fields in ((0, range(4)), (1, (4,))):
            packed = jnp.zeros((8, 128), f32)
            for f in fields:
                for j in range(4):
                    p = 4 * (f % 4) + j
                    at = pl.multiple_of(row(f, i, j, 0) + 24 * side, 8)
                    packed = jnp.where(spot == p, pltpu.roll(q[pl.ds(at, 8), :], (120 + p) % 128, 1), packed)
            message[pl.ds(80 + block * 32 + i * 8, 8), :] = pltpu.roll(packed, side, 1)


def pack_blocks(q, m, side, message):
    place = ((lane_ids() >> 4) + side) & 7
    for g in range(10):
        packed = jnp.zeros((8, 128), f32)
        for p in range(8):
            f, n = divmod(g * 8 + p, 16)
            i, k = divmod(n, 4)
            at = pl.multiple_of(row(f, i, 0, k) + 96 * side, 8)
            packed = jnp.where(place == p, pltpu.roll(q[pl.ds(at, 8), :], 16 * p, 1), packed)
        message[pl.ds(g * 8, 8), :] = pltpu.roll(packed, 16 * side, 1)
    message[pl.ds(80, 8), :] = pltpu.roll(m[pl.ds(8, 8), :], 16 * side, 1)


def choose_sectors(par, ga0, ga1, back, ahead):
    rows = pl.ds(0, back.shape[0])
    one, two = ga0[rows, :], ga1[rows, :]
    back[...] = jnp.where(par[0] == 0, two, one)
    ahead[...] = jnp.where(par[0] == 0, one, two)


def choose_blocks(par, gr0, gr1, below, above):
    rows = pl.ds(0, below.shape[0])
    one, two = gr0[rows, :], gr1[rows, :]
    below[...] = jnp.where(par[2] == 0, 0.0, jnp.where(par[1] == 0, two, one))
    above[...] = jnp.where(par[2] == 7, 0.0, jnp.where(par[1] == 0, one, two))


def sector_jumps(back, ahead, mortar):
    sub = lax.broadcasted_iota(jnp.int32, (8, 128), 0)
    axial = lane_ids() & 15

    def az(f, j, k, x0, x3):
        at = pl.ds(f * 16 + 4 * j + k, 1)
        return jnp.where(sub == 0, back[at, :] - x0, 0.0), jnp.where(sub == 7, ahead[at, :] - x3, 0.0)

    def ax(f, i, j, x0, x3):
        to_stator, to_rotor = mortar(f, i, j)
        return jnp.where(axial == 8, to_stator, 0.0), jnp.where(axial == 7, to_rotor, 0.0)

    return {0: az, 2: ax}


def rim_jumps(below, above):
    lanes = lane_ids()

    def rad(f, i, k, x0, x3):
        at = pl.ds(f * 16 + 4 * i + k, 1)
        before = pltpu.roll(jnp.broadcast_to(below[at, :], (8, 128)), 16, 1, stride=16, stride_axis=0)
        after = pltpu.roll(jnp.broadcast_to(above[at, :], (8, 128)), 0, 1, stride=16, stride_axis=0)
        return jnp.where(lanes < 16, before - x0, 0.0), jnp.where(lanes >= 112, after - x3, 0.0)

    return rad


def block_jumps(below, above, owed):
    lanes = lane_ids()
    m_below = below[pl.ds(80, 8), :]
    m_above = pltpu.roll(above[pl.ds(80, 8), :], 112, 1)

    def rad(f, i, k, x0, x3):
        n = f * 16 + 4 * i + k
        g, p = divmod(n, 8)
        at = pl.ds(g * 8, 8)
        before = pltpu.roll(below[at, :], (128 - 16 * p) % 128, 1) + m_below * owed[pl.ds(n * 16, 8), :]
        after = pltpu.roll(above[at, :], (112 - 16 * p) % 128, 1) + m_above * owed[pl.ds(n * 16 + 8, 8), :]
        return jnp.where(lanes < 16, before - x0, 0.0), jnp.where(lanes >= 112, after - x3, 0.0)

    return rad


def mortar_matrix(lists, following, tables):
    own, later = lists.T, following.T

    def column(t):
        return jnp.concatenate(
            [own[0:8, 2 * t : 2 * t + 1], own[0:8, 2 * t + 1 : 2 * t + 2], later[0:8, 2 * t : 2 * t + 1]], axis=0
        )

    rotor, stator, kind = (column(t) for t in range(3))
    slot = lax.broadcasted_iota(jnp.int32, (24, 1), 0)
    filled = jnp.concatenate(
        [
            jnp.broadcast_to(lists[6:7, 0:1], (8, 1)),
            jnp.broadcast_to(lists[7:8, 0:1], (8, 1)),
            jnp.broadcast_to(following[6:7, 0:1], (8, 1)),
        ],
        axis=0,
    )
    used = ((slot & 7).astype(f32) < filled).astype(f32)
    lanes = lax.broadcasted_iota(jnp.int32, (24, 128), 1)
    pick = (lanes.astype(f32) == kind).astype(f32)
    face = (lanes & 7).astype(f32)
    on_rotor = (face == rotor).astype(f32)
    on_stator = (face == stator).astype(f32) * 1.0
    entries = jnp.dot(pick, tables, precision=highest, preferred_element_type=f32)
    order = lax.broadcasted_iota(jnp.int32, (24, 128), 0)
    p_rot = entries[:, 0:128] * on_rotor
    p_sta = -entries[:, 128:256] * on_stator
    q_rot = -entries[:, 256:384] * on_rotor * used
    q_sta = entries[:, 384:512] * on_stator * used
    first = (order < 8).astype(f32)
    third = (order >= 16).astype(f32)
    b_parts = [p_rot * first, p_rot * (1.0 - first), p_sta * (1.0 - third), p_sta * third]
    c_parts = [q_sta * (1.0 - third), q_rot * (1.0 - first)]
    b_all = jnp.concatenate(
        [jnp.concatenate([b[:, 32 * m : 32 * m + 32] for b in b_parts], axis=1) for m in range(4)], axis=0
    )
    c_all = jnp.concatenate(
        [jnp.concatenate([c[:, 32 * m : 32 * m + 32] for c in c_parts], axis=1) for m in range(4)], axis=0
    )
    return lax.dot_general(
        c_all, b_all, (((0,), (0,)), ((), ())), precision=highest, preferred_element_type=f32
    )


def mortar_terms(par, matrix, s0, s1, back, ahead, placed):
    even = par[0] == 0
    blocks = []
    for block in range(2):
        at = pl.ds(80 + block * 32, 32)
        one, two = s0[at, :], s1[at, :]
        mine, yours = jnp.where(even, one, two), jnp.where(even, two, one)
        blocks.append(jnp.concatenate([back[at, :], mine, yours, ahead[at, :]], axis=0))
    traces = jnp.concatenate(blocks, axis=1)
    placed[...] = jnp.dot(matrix, traces, precision=highest, preferred_element_type=f32)

    def mortar(f, i, j):
        block, p = divmod(4 * f + j, 16)
        at = pl.ds(128 * block, 128)
        to_stator = pltpu.roll(placed[pl.ds(8 * i, 8), at], (8 - p) % 128, 1)
        to_rotor = pltpu.roll(placed[pl.ds(32 + 8 * i, 8), at], (7 - p) % 128, 1)
        return to_stator, to_rotor

    return mortar


def rim_rows(pieces, side, message):
    for c in (0, 128, 256):
        width = min(128, 320 - c)
        block = jnp.concatenate([pieces(7 - a, c, width) for a in range(8)], axis=0).T
        for g in range(width // 16):
            at = 16 * g
            chosen = jnp.where(side == 0, block[at : at + 4], block[at + 12 : at + 16])
            message[pl.ds(c // 4 + 4 * g, 4), :] = chosen


def rim_message(nat, side, message):
    start = pl.multiple_of(112 * side, 16)
    rim_rows(lambda a, c, width: nat[a, pl.ds(start, 16), c : c + width], side, message)


def enter_kernel(state, nat, q, sems):
    copies = [pltpu.make_async_copy(state.at[a], nat.at[a], sems.at[a]) for a in range(8)]
    for copy in copies:
        copy.start()
    for a in range(8):
        copies[a].wait()
        for c in (0, 128, 256):
            width = min(128, 320 - c)
            q[pl.ds(c * 8 + a, width, stride=8), :] = nat[a, :, c : c + width].T


def first_kernel(counts, q, slots, inner, s1):
    pack_sector(q, position()[0], s1)
    used = jnp.concatenate(
        [jnp.broadcast_to(counts[:, b : b + 1].astype(f32), (1, 8)) for b in range(2)], axis=0
    )
    lists = jnp.concatenate([slots[t].astype(f32) for t in range(3)] + [used], axis=0)
    s1[pl.ds(144, 8), :] = jnp.concatenate([lists, jnp.zeros((8, 120), f32)], axis=1)


def rim_kernel(nat, s1, r1):
    rim_message(nat, position()[1], r1)


def others_kernel(nat, q, s1, r1, s0, r0):
    par = position()
    rim_message(nat, 1 - par[1], r0)
    pack_sector(q, 1 - par[0], s0)
    s0[pl.ds(144, 8), :] = s1[pl.ds(144, 8), :]


def ahead_kernel(q, m, counts, slots, acc):
    @pl.when(position()[3] < 16)
    def _():
        inner_operator(q, m, acc, lambda x, *at: x)


def inner_kernel(q, m, early, acc):
    before = position()[3] < 16

    @pl.when(before)
    def _():
        acc[...] = early[...]

    @pl.when(jnp.logical_not(before))
    def _():
        inner_operator(q, m, acc, lambda x, *at: x)


def middle_kernel(inner, q, m, s0, s1, tables, ga0, ga1, part, matrix, r1, placed, back, ahead):
    par = position()
    choose_sectors(par, ga0, ga1, back, ahead)
    matrix[...] = mortar_matrix(s1[pl.ds(144, 8), :], ahead[pl.ds(144, 8), :], tables[...])
    mortar = mortar_terms(par, matrix[...], s0, s1, back, ahead, placed)
    end_terms(q, m, inner, part, 1.0, range(5), sector_jumps(back, ahead, mortar), (2, 0))
    pack_blocks(part, m, par[1], r1)
    pad = r1.shape[0] - 88
    if pad:
        r1[pl.ds(88, pad), :] = jnp.zeros((pad, 128), f32)


def block_kernel(part, q, m, gr0, gr1, s, owed, below, above):
    choose_blocks(position(), gr0, gr1, below, above)
    rad = rim_jumps(below, above)
    scale = 3.0 * m[pl.ds(8, 8), :]
    for f in range(5):
        for i in range(4):
            at = pl.ds(row(f, i, 1, 0), 64)
            s[at, :] = part[at, :]

    def fetch(i, k):
        return ([rad(f, i, k, tile(q, f, i, 0, k), tile(q, f, i, 3, k)) for f in range(5)],)

    def finish(i, k, jumps):
        for f in range(5):
            other = coupled(f, 1)
            low, high = jumps[f]
            lower, upper = (low, high) if other is None else (low + jumps[other][0], high - jumps[other][1])
            theirs, yours = (low, high) if other is None else (low - jumps[other][0], high + jumps[other][1])
            for j, term in ((0, lower), (3, upper)):
                at = pl.ds(row(f, i, j, k), 8)
                s[at, :] = part[at, :] + scale * term
            n = f * 16 + 4 * i + k
            owed[pl.ds(n * 16, 8), :] = -3.0 * theirs
            owed[pl.ds(n * 16 + 8, 8), :] = -3.0 * yours

    staged(pairs(), fetch, finish)


def sector_kernel(s, s1):
    par = position()
    pack_sector(s, par[0], s1)
    s1[pl.ds(144, 8), :] = jnp.zeros((8, 128), f32)


def later_kernel(s, part, m, s0, r0):
    par = position()
    pack_blocks(part, m, 1 - par[1], r0)
    pack_sector(s, 1 - par[0], s0)


def inner_last_kernel(s, m, q, acc):
    half = {8 * d: 0.5 * m[pl.ds(8 * d, 8), :] for d in range(3)}

    class Halved:
        def __getitem__(self, at):
            return half[at[0].start]

    inner_operator(s, Halved(), acc, lambda x, *at: 0.5 * (x + tile(q, *at)))


def last_kernel(
    inner, s, m, s0, s1, matrix, owed, ga0, ga1, gr0, gr1, out, acc, placed, back, ahead, below, above, turned, sems
):
    par = position()
    choose_sectors(par, ga0, ga1, back, ahead)
    choose_blocks(par, gr0, gr1, below, above)
    mortar = mortar_terms(par, matrix[...], s0, s1, back, ahead, placed)
    jumps = sector_jumps(back, ahead, mortar)
    jumps[1] = block_jumps(below, above, owed)
    copies = []
    for c, fields in ((128, (2, 3)), (0, (0, 1)), (256, (4,))):
        width = min(128, 320 - c)
        end_terms(s, m, inner, acc, 0.5, fields, jumps)
        for a in range(8):
            turned[a, :, c : c + width] = acc[pl.ds(c * 8 + a, width, stride=8), :].T
            copies.append(
                pltpu.make_async_copy(
                    turned.at[a, :, pl.ds(c, width)], out.at[a, :, pl.ds(c, width)], sems.at[len(copies)]
                )
            )
            copies[-1].start()
    for copy in copies:
        copy.wait()


def call(kernel, outs, scratch=(), where={}, out_where=pltpu.VMEM, limit=32, cost=1):
    def run(*args):
        return pl.pallas_call(
            kernel,
            out_shape=[jax.ShapeDtypeStruct(s, f32) for s in outs],
            in_specs=[pl.BlockSpec(memory_space=where.get(n, pltpu.VMEM)) for n in range(len(args))],
            out_specs=[pl.BlockSpec(memory_space=out_where)] * len(outs),
            scratch_shapes=[s if not isinstance(s, tuple) else pltpu.VMEM(s, f32) for s in scratch],
            compiler_params=pltpu.CompilerParams(vmem_limit_bytes=limit * 2**20),
            cost_estimate=pl.CostEstimate(flops=0, transcendentals=0, bytes_accessed=cost * 3_000_000),
        )(*args)

    return run


def pairings(sectors, blocks):
    at = lambda a, r: (a % sectors) * blocks + r
    az0 = [(a, a ^ 1) for a in range(sectors)]
    az1 = [(a, (a + 1 if a % 2 else a - 1) % sectors) for a in range(sectors)]
    rad0 = [(r, r ^ 1) for r in range(blocks)]
    rad1 = []
    for a in range(sectors):
        for r in range(blocks):
            if r in (0, blocks - 1):
                rad1.append((at(a, r), at(a ^ 1, r)))
            else:
                rad1.append((at(a, r), at(a, r + 1 if r % 2 else r - 1)))
    return az0, az1, rad0, rad1


def shards(solution, metric, intersections, counts, projections):
    sectors, blocks = lax.axis_size("azim"), lax.axis_size("radax")
    az0, az1, rad0, rad1 = pairings(sectors, blocks)

    def across(r0, r1, s0, s1):
        gr1 = lax.ppermute(r1, ("azim", "radax"), rad1)
        gs1 = lax.ppermute(s1, "azim", az1)
        gr0 = lax.ppermute(r0, "radax", rad0)
        gs0 = lax.ppermute(s0, "azim", az0)
        return gs0, gs1, gr0, gr1

    state, rim, trace, first_trace = (2560, 128), (80, 128), (144, 128), (152, 128)
    dma = pltpu.SemaphoreType.DMA
    turned = jnp.concatenate([projections[:2], projections[2:].transpose(0, 1, 3, 2)], axis=0)
    tables = jnp.repeat(turned.transpose(1, 0, 2, 3).reshape(16, 64), 8, axis=1)
    tables = jnp.pad(tables, ((0, 112), (0, 0)))
    m = time_step * metric.transpose(3, 0, 1, 2).reshape(24, 128)
    nat, q = call(enter_kernel, [(8, 128, 320), state], [dma((8,))], {0: pltpu.HBM}, limit=50)(
        solution.reshape(8, 128, 320)
    )
    slots = intersections.transpose(0, 2, 1, 3)[0]
    (early,) = call(ahead_kernel, [state])(q, m, counts, slots)
    (s1,) = call(first_kernel, [first_trace])(counts, q, slots, early)
    (r1,) = call(rim_kernel, [rim])(nat, s1)
    s0, r0 = call(others_kernel, [first_trace, rim])(nat, q, s1, r1)
    ga0, ga1, gr0, gr1 = across(r0, r1, s0, s1)
    (inner,) = call(inner_kernel, [state])(q, m, early)
    part, matrix, r1 = call(
        middle_kernel, [state, (64, 128), (160, 128)], [(64, 256), first_trace, first_trace]
    )(inner, q, m, s0, s1, tables, ga0, ga1)
    s, owed = call(block_kernel, [state, (1280, 128)], [rim, rim])(part, q, m, gr0, gr1)
    (s1,) = call(sector_kernel, [first_trace])(s)
    s0, r0 = call(later_kernel, [trace, (88, 128)])(s, part, m)
    got = across(r0, r1, s0, s1)
    (inner,) = call(inner_last_kernel, [state])(s, m, q)
    sides = [state, (64, 256), trace, trace, (88, 128), (88, 128)]
    (out,) = call(last_kernel, [(8, 128, 320)], sides + [(8, 128, 320), dma((24,))], {}, pltpu.HBM)(
        inner, s, m, s0, s1, matrix, owed, *got
    )
    return out.reshape(solution.shape)


def solution(mesh):
    in_specs = (
        P("azim", "radax", None, None),
        P("azim", "radax", None, None),
        P("azim", None, None, None),
        P("azim", None),
        P(),
    )
    out_specs = P("azim", "radax", None, None)
    return jax.shard_map(shards, mesh=mesh, in_specs=in_specs, out_specs=out_specs, check_vma=False)
```

```python
import functools
import jax
import jax.numpy as jnp
import numpy as np
from jax import lax
from jax.experimental import pallas as pl
from jax.experimental.pallas import tpu as pltpu
from jax.sharding import PartitionSpec as P

time_step = 0.02
mean_flow = (0.5, 0.0, 0.4)
speeds = tuple(abs(u) + 1.0 for u in mean_flow)
highest = lax.Precision.HIGHEST
f32 = jnp.float32


def line_numbers():
    points = np.array([-1.0, -1.0 / np.sqrt(5.0), 1.0 / np.sqrt(5.0), 1.0])
    barycentric = np.array(
        [1.0 / np.prod([points[j] - points[k] for k in range(4) if k != j]) for j in range(4)]
    )
    single = np.zeros((4, 4))
    for i in range(4):
        for j in range(4):
            if i != j:
                single[i, j] = barycentric[j] / barycentric[i] / (points[i] - points[j])
        single[i, i] = -np.sum(single[i])
    return single


D = line_numbers()


def row(f, i, j, k):
    return (f * 64 + 16 * i + 4 * j + k) * 8


def tile(ref, f, i, j, k):
    return ref[pl.ds(row(f, i, j, k), 8), :]


def lane_ids():
    return lax.broadcasted_iota(jnp.int32, (8, 128), 1)


def minus_slope(x, scale):
    e0, e1 = x[0] - x[3], x[1] - x[2]
    t = (x[0] + x[3]) - (x[1] + x[2])
    c = -scale * 0.5
    outer = (c * (D[0, 0] - D[0, 3])) * e0 + (c * (D[0, 1] - D[0, 2])) * e1
    inner = (c * (D[1, 0] - D[1, 3])) * e0 + (c * (D[1, 1] - D[1, 2])) * e1
    outer_t = (c * (D[0, 0] + D[0, 3])) * t
    inner_t = (c * (D[1, 0] + D[1, 3])) * t
    return [outer + outer_t, inner + inner_t, inner - inner_t, outer - outer_t]


def line_terms(d, x, low, high):
    flow, speed = mean_flow[d], speeds[d]
    w0 = [3.0 * v for v in low]
    w3 = [3.0 * v for v in high]
    mine = 1 + d
    slopes = {}
    for f in (mine, 4):
        h = minus_slope(x[f], 1.0)
        h[0] = h[0] + w0[f]
        h[3] = h[3] - w3[f]
        slopes[f] = h
    result = []
    for f in range(5):
        if f == mine:
            r = [slopes[4][i] + flow * slopes[mine][i] if flow else slopes[4][i] for i in range(4)]
            r[0] = r[0] + speed * w0[f]
            r[3] = r[3] + speed * w3[f]
        elif f == 4:
            r = [slopes[mine][i] + flow * slopes[4][i] if flow else slopes[mine][i] for i in range(4)]
            r[0] = r[0] + speed * w0[f]
            r[3] = r[3] + speed * w3[f]
        else:
            r = minus_slope(x[f], flow) if flow else [None] * 4
            if f == 0:
                r = [slopes[mine][i] if r[i] is None else r[i] + slopes[mine][i] for i in range(4)]
            lows, highs = (speed + flow) * w0[f], (speed - flow) * w3[f]
            r[0] = lows if r[0] is None else r[0] + lows
            r[3] = highs if r[3] is None else r[3] + highs
        result.append(r)
    return result


def position():
    azim, radax = lax.axis_index("azim"), lax.axis_index("radax")
    return azim & 1, radax & 1, radax, azim


def staged(lines, fetch, finish):
    ready = fetch(*lines[0])
    for at, line in enumerate(lines):
        later = fetch(*lines[at + 1]) if at + 1 < len(lines) else None
        finish(*line, *ready)
        ready = later


def pairs():
    return [(p, r) for p in range(4) for r in range(4)]


def inner_operator(q, m, acc, first):
    lanes = lane_ids()
    sub = lax.broadcasted_iota(jnp.int32, (8, 128), 0)
    axial = lanes & 15

    def passes(d, nodes, low_of, high_of, put):
        scale = m[pl.ds(8 * d, 8), :]

        def fetch(p, r):
            low, high = [], []
            for f in range(5):
                x0, x3 = tile(q, f, *nodes(p, r, 0)), tile(q, f, *nodes(p, r, 3))
                low.append(low_of(x0, x3))
                high.append(high_of(x0, x3))
            return low, high

        def finish(p, r, low, high):
            x = [[tile(q, f, *nodes(p, r, e)) for e in range(4)] for f in range(5)]
            terms = line_terms(d, x, low, high)
            for f in range(5):
                for e in range(4):
                    if terms[f][e] is not None:
                        put(f, *nodes(p, r, e), x[f][e], scale * terms[f][e])

        staged(pairs(), fetch, finish)

    def begin(f, i, j, k, x, term):
        acc[pl.ds(row(f, i, j, k), 8), :] = first(x, f, i, j, k) + term

    def add(f, i, j, k, x, term):
        at = pl.ds(row(f, i, j, k), 8)
        acc[at, :] = acc[at, :] + term

    def axial_low(x0, x3):
        outside = jnp.where(axial == 0, 0.0, pltpu.roll(x3, 1, 1))
        return jnp.where(axial == 8, 0.0, outside - x0)

    def axial_high(x0, x3):
        outside = jnp.where(axial == 15, 0.0, pltpu.roll(x0, 127, 1))
        return jnp.where(axial == 7, 0.0, outside - x3)

    passes(2, lambda i, j, k: (i, j, k), axial_low, axial_high, begin)
    passes(
        0,
        lambda j, k, i: (i, j, k),
        lambda x0, x3: jnp.where(sub == 0, 0.0, pltpu.roll(x3, 1, 0) - x0),
        lambda x0, x3: jnp.where(sub == 7, 0.0, pltpu.roll(x0, 7, 0) - x3),
        add,
    )
    passes(
        1,
        lambda i, k, j: (i, j, k),
        lambda x0, x3: jnp.where(lanes < 16, 0.0, pltpu.roll(x3, 16, 1) - x0),
        lambda x0, x3: jnp.where(lanes >= 112, 0.0, pltpu.roll(x0, 112, 1) - x3),
        add,
    )


def coupled(f, d):
    return 4 if f == 1 + d else 1 + d if f in (0, 4) else None


def end_terms(q, m, base, acc, factor, fields, sides, directions=(2, 0, 1)):
    for f in fields:
        for i, j in pairs():
            at = pl.ds(row(f, i, j, 1), 16)
            acc[at, :] = base[at, :]
    for d in directions:
        nodes = (lambda j, k, i: (i, j, k), lambda i, k, j: (i, j, k), lambda i, j, k: (i, j, k))[d]
        scale = (3.0 * factor) * m[pl.ds(8 * d, 8), :]
        flow, speed = mean_flow[d], speeds[d]
        old = base if d == 2 else acc
        needed = sorted(set(fields) | {coupled(f, d) for f in fields} - {None})

        def fetch(p, r):
            return ({f: sides[d](f, p, r, tile(q, f, *nodes(p, r, 0)), tile(q, f, *nodes(p, r, 3))) for f in needed},)

        def finish(p, r, jumps):
            for f in fields:
                other = coupled(f, d)
                for end, sign in ((0, 1.0), (1, -1.0)):
                    term = (speed + sign * flow) * jumps[f][end]
                    if other is not None:
                        term = term + jumps[other][end] if end == 0 else term - jumps[other][end]
                    at = pl.ds(row(f, *nodes(p, r, 3 * end)), 8)
                    acc[at, :] = old[at, :] + scale * term

        staged(pairs(), fetch, finish)


def pack_sector(q, side, message):
    spot = (lane_ids() + side) & 15
    for f in range(5):
        low = q[pl.ds(f * 64 * 8, 16, stride=8), :]
        high = q[pl.ds((f * 64 + 48) * 8 + 7, 16, stride=8), :]
        message[pl.ds(f * 16, 16), :] = jnp.where(side == 0, low, high)
    for group in range(5):
        packed = jnp.zeros((8, 128), f32)
        for p in range(16):
            f, i, j = (p // 4, group, p % 4) if group < 4 else (4, p // 4, p % 4)
            at = pl.multiple_of(row(f, i, j, 0) + 24 * side, 8)
            packed = jnp.where(spot == p, pltpu.roll(q[pl.ds(at, 8), :], (120 + p) % 128, 1), packed)
        message[pl.ds(80 + group * 8, 8), :] = pltpu.roll(packed, side, 1)


def pack_blocks(q, m, side, message):
    place = ((lane_ids() >> 4) + side) & 7
    for g in range(10):
        packed = jnp.zeros((8, 128), f32)
        for p in range(8):
            f, n = divmod(g * 8 + p, 16)
            i, k = divmod(n, 4)
            at = pl.multiple_of(row(f, i, 0, k) + 96 * side, 8)
            packed = jnp.where(place == p, pltpu.roll(q[pl.ds(at, 8), :], 16 * p, 1), packed)
        message[pl.ds(g * 8, 8), :] = pltpu.roll(packed, 16 * side, 1)
    message[pl.ds(80, 8), :] = pltpu.roll(m[pl.ds(8, 8), :], 16 * side, 1)


def choose_sectors(par, ga0, ga1, back, ahead):
    rows = pl.ds(0, back.shape[0])
    one, two = ga0[rows, :], ga1[rows, :]
    back[...] = jnp.where(par[0] == 0, two, one)
    ahead[...] = jnp.where(par[0] == 0, one, two)


def choose_blocks(par, gr0, gr1, below, above):
    rows = pl.ds(0, below.shape[0])
    one, two = gr0[rows, :], gr1[rows, :]
    below[...] = jnp.where(par[2] == 0, 0.0, jnp.where(par[1] == 0, two, one))
    above[...] = jnp.where(par[2] == 7, 0.0, jnp.where(par[1] == 0, one, two))


def sector_jumps(back, ahead, mortar):
    sub = lax.broadcasted_iota(jnp.int32, (8, 128), 0)
    axial = lane_ids() & 15

    def az(f, j, k, x0, x3):
        at = pl.ds(f * 16 + 4 * j + k, 1)
        return jnp.where(sub == 0, back[at, :] - x0, 0.0), jnp.where(sub == 7, ahead[at, :] - x3, 0.0)

    def ax(f, i, j, x0, x3):
        to_stator, to_rotor = mortar(f, i, j)
        return jnp.where(axial == 8, to_stator, 0.0), jnp.where(axial == 7, to_rotor, 0.0)

    return {0: az, 2: ax}


def rim_jumps(below, above):
    lanes = lane_ids()

    def rad(f, i, k, x0, x3):
        at = pl.ds(f * 16 + 4 * i + k, 1)
        before = pltpu.roll(jnp.broadcast_to(below[at, :], (8, 128)), 16, 1, stride=16, stride_axis=0)
        after = pltpu.roll(jnp.broadcast_to(above[at, :], (8, 128)), 0, 1, stride=16, stride_axis=0)
        return jnp.where(lanes < 16, before - x0, 0.0), jnp.where(lanes >= 112, after - x3, 0.0)

    return rad


def block_jumps(below, above, owed):
    lanes = lane_ids()
    m_below = below[pl.ds(80, 8), :]
    m_above = pltpu.roll(above[pl.ds(80, 8), :], 112, 1)

    def rad(f, i, k, x0, x3):
        n = f * 16 + 4 * i + k
        g, p = divmod(n, 8)
        at = pl.ds(g * 8, 8)
        before = pltpu.roll(below[at, :], (128 - 16 * p) % 128, 1) + m_below * owed[pl.ds(n * 16, 8), :]
        after = pltpu.roll(above[at, :], (112 - 16 * p) % 128, 1) + m_above * owed[pl.ds(n * 16 + 8, 8), :]
        return jnp.where(lanes < 16, before - x0, 0.0), jnp.where(lanes >= 112, after - x3, 0.0)

    return rad


def mortar_matrix(lists, following, tables):
    own, later = lists.T, following.T

    def column(t):
        return jnp.concatenate(
            [own[0:8, 2 * t : 2 * t + 1], own[0:8, 2 * t + 1 : 2 * t + 2], later[0:8, 2 * t : 2 * t + 1]], axis=0
        )

    rotor, stator, kind = (column(t) for t in range(3))
    slot = lax.broadcasted_iota(jnp.int32, (24, 1), 0)
    filled = jnp.concatenate(
        [
            jnp.broadcast_to(lists[6:7, 0:1], (8, 1)),
            jnp.broadcast_to(lists[7:8, 0:1], (8, 1)),
            jnp.broadcast_to(following[6:7, 0:1], (8, 1)),
        ],
        axis=0,
    )
    used = ((slot & 7).astype(f32) < filled).astype(f32)
    lanes = lax.broadcasted_iota(jnp.int32, (24, 128), 1)
    pick = (lanes.astype(f32) == kind).astype(f32)
    face = (lanes & 7).astype(f32)
    on_rotor = (face == rotor).astype(f32)
    on_stator = (face == stator).astype(f32) * 1.0
    entries = jnp.dot(pick, tables, precision=highest, preferred_element_type=f32)
    order = lax.broadcasted_iota(jnp.int32, (24, 128), 0)
    p_rot = entries[:, 0:128] * on_rotor
    p_sta = -entries[:, 128:256] * on_stator
    q_rot = -entries[:, 256:384] * on_rotor * used
    q_sta = entries[:, 384:512] * on_stator * used
    first = (order < 8).astype(f32)
    third = (order >= 16).astype(f32)
    b_parts = [p_rot * first, p_rot * (1.0 - first), p_sta * (1.0 - third), p_sta * third]
    c_parts = [q_sta * (1.0 - third), q_rot * (1.0 - first)]
    b_all = jnp.concatenate(
        [jnp.concatenate([b[:, 32 * m : 32 * m + 32] for b in b_parts], axis=1) for m in range(4)], axis=0
    )
    c_all = jnp.concatenate(
        [jnp.concatenate([c[:, 32 * m : 32 * m + 32] for c in c_parts], axis=1) for m in range(4)], axis=0
    )
    return lax.dot_general(
        c_all, b_all, (((0,), (0,)), ((), ())), precision=highest, preferred_element_type=f32
    )


def mortar_terms(par, matrix, s0, s1, back, ahead, placed):
    even = par[0] == 0

    def four(ref):
        return ref[pl.ds(80, 32), :]

    def fifth(ref):
        packed = ref[pl.ds(112, 8), :]
        return jnp.concatenate([packed] + [pltpu.roll(packed, 128 - 4 * i, 1) for i in range(1, 4)], axis=0)

    blocks = []
    for part in (four, fifth):
        one, two = part(s0), part(s1)
        mine, yours = jnp.where(even, one, two), jnp.where(even, two, one)
        blocks.append(jnp.concatenate([part(back), mine, yours, part(ahead)], axis=0))
    traces = jnp.concatenate(blocks, axis=1)
    placed[...] = jnp.dot(matrix, traces, precision=highest, preferred_element_type=f32)

    def mortar(f, i, j):
        block, p = divmod(4 * f + j, 16)
        at = pl.ds(128 * block, 128)
        to_stator = pltpu.roll(placed[pl.ds(8 * i, 8), at], (8 - p) % 128, 1)
        to_rotor = pltpu.roll(placed[pl.ds(32 + 8 * i, 8), at], (7 - p) % 128, 1)
        return to_stator, to_rotor

    return mortar


def rim_rows(pieces, side, message):
    for c in (0, 128, 256):
        width = min(128, 320 - c)
        block = jnp.concatenate([pieces(7 - a, c, width) for a in range(8)], axis=0).T
        for g in range(width // 16):
            at = 16 * g
            chosen = jnp.where(side == 0, block[at : at + 4], block[at + 12 : at + 16])
            message[pl.ds(c // 4 + 4 * g, 4), :] = chosen


def rim_message(nat, side, message):
    start = pl.multiple_of(112 * side, 16)
    rim_rows(lambda a, c, width: nat[a, pl.ds(start, 16), c : c + width], side, message)


def enter_kernel(state, nat, q, sems):
    copies = [pltpu.make_async_copy(state.at[a], nat.at[a], sems.at[a]) for a in range(8)]
    for copy in copies:
        copy.start()
    for a in range(8):
        copies[a].wait()
        for c in (0, 128, 256):
            width = min(128, 320 - c)
            q[pl.ds(c * 8 + a, width, stride=8), :] = nat[a, :, c : c + width].T


def first_kernel(counts, q, slots, inner, s1):
    pack_sector(q, position()[0], s1)
    used = jnp.concatenate(
        [jnp.broadcast_to(counts[:, b : b + 1].astype(f32), (1, 8)) for b in range(2)], axis=0
    )
    lists = jnp.concatenate([slots[t].astype(f32) for t in range(3)] + [used], axis=0)
    s1[pl.ds(120, 8), :] = jnp.concatenate([lists, jnp.zeros((8, 120), f32)], axis=1)


def rim_kernel(nat, s1, r1):
    rim_message(nat, position()[1], r1)


def others_kernel(q, s1, r1, s0):
    pack_sector(q, 1 - position()[0], s0)
    s0[pl.ds(120, 8), :] = s1[pl.ds(120, 8), :]


def other_rim_kernel(nat, s0, r0):
    rim_message(nat, 1 - position()[1], r0)


def ahead_kernel(q, m, counts, slots, acc):
    @pl.when(position()[3] < 16)
    def _():
        inner_operator(q, m, acc, lambda x, *at: x)


def inner_kernel(q, m, early, acc):
    before = position()[3] < 16

    @pl.when(before)
    def _():
        acc[...] = early[...]

    @pl.when(jnp.logical_not(before))
    def _():
        inner_operator(q, m, acc, lambda x, *at: x)


def middle_kernel(inner, q, m, s0, s1, tables, ga0, ga1, part, matrix, r1, placed, back, ahead):
    par = position()
    choose_sectors(par, ga0, ga1, back, ahead)
    matrix[...] = mortar_matrix(s1[pl.ds(120, 8), :], ahead[pl.ds(120, 8), :], tables[...])
    mortar = mortar_terms(par, matrix[...], s0, s1, back, ahead, placed)
    end_terms(q, m, inner, part, 1.0, range(5), sector_jumps(back, ahead, mortar), (2, 0))
    pack_blocks(part, m, par[1], r1)
    pad = r1.shape[0] - 88
    if pad:
        r1[pl.ds(88, pad), :] = jnp.zeros((pad, 128), f32)


def block_kernel(part, q, m, gr0, gr1, s, owed, below, above):
    choose_blocks(position(), gr0, gr1, below, above)
    rad = rim_jumps(below, above)
    scale = 3.0 * m[pl.ds(8, 8), :]
    for f in range(5):
        for i in range(4):
            at = pl.ds(row(f, i, 1, 0), 64)
            s[at, :] = part[at, :]

    def fetch(i, k):
        return ([rad(f, i, k, tile(q, f, i, 0, k), tile(q, f, i, 3, k)) for f in range(5)],)

    def finish(i, k, jumps):
        for f in range(5):
            other = coupled(f, 1)
            low, high = jumps[f]
            lower, upper = (low, high) if other is None else (low + jumps[other][0], high - jumps[other][1])
            theirs, yours = (low, high) if other is None else (low - jumps[other][0], high + jumps[other][1])
            for j, term in ((0, lower), (3, upper)):
                at = pl.ds(row(f, i, j, k), 8)
                s[at, :] = part[at, :] + scale * term
            n = f * 16 + 4 * i + k
            owed[pl.ds(n * 16, 8), :] = -3.0 * theirs
            owed[pl.ds(n * 16 + 8, 8), :] = -3.0 * yours

    staged(pairs(), fetch, finish)


def sector_kernel(s, s1):
    par = position()
    pack_sector(s, par[0], s1)
    s1[pl.ds(120, 8), :] = jnp.zeros((8, 128), f32)


def later_kernel(s, part, m, s0, r0):
    par = position()
    pack_blocks(part, m, 1 - par[1], r0)
    pack_sector(s, 1 - par[0], s0)


def inner_last_kernel(s, m, q, acc):
    half = {8 * d: 0.5 * m[pl.ds(8 * d, 8), :] for d in range(3)}

    class Halved:
        def __getitem__(self, at):
            return half[at[0].start]

    inner_operator(s, Halved(), acc, lambda x, *at: 0.5 * (x + tile(q, *at)))


def last_kernel(
    inner, s, m, s0, s1, matrix, owed, ga0, ga1, gr0, gr1, out, acc, placed, back, ahead, below, above, turned, sems
):
    par = position()
    choose_sectors(par, ga0, ga1, back, ahead)
    choose_blocks(par, gr0, gr1, below, above)
    mortar = mortar_terms(par, matrix[...], s0, s1, back, ahead, placed)
    jumps = sector_jumps(back, ahead, mortar)
    jumps[1] = block_jumps(below, above, owed)
    copies = []
    for c, fields in ((128, (2, 3)), (0, (0, 1)), (256, (4,))):
        width = min(128, 320 - c)
        end_terms(s, m, inner, acc, 0.5, fields, jumps)
        for a in range(8):
            turned[a, :, c : c + width] = acc[pl.ds(c * 8 + a, width, stride=8), :].T
            copies.append(
                pltpu.make_async_copy(
                    turned.at[a, :, pl.ds(c, width)], out.at[a, :, pl.ds(c, width)], sems.at[len(copies)]
                )
            )
            copies[-1].start()
    for copy in copies:
        copy.wait()


def call(kernel, outs, scratch=(), where={}, out_where=pltpu.VMEM, limit=32, cost=1):
    def run(*args):
        return pl.pallas_call(
            kernel,
            out_shape=[jax.ShapeDtypeStruct(s, f32) for s in outs],
            in_specs=[pl.BlockSpec(memory_space=where.get(n, pltpu.VMEM)) for n in range(len(args))],
            out_specs=[pl.BlockSpec(memory_space=out_where)] * len(outs),
            scratch_shapes=[s if not isinstance(s, tuple) else pltpu.VMEM(s, f32) for s in scratch],
            compiler_params=pltpu.CompilerParams(vmem_limit_bytes=limit * 2**20),
            cost_estimate=pl.CostEstimate(flops=0, transcendentals=0, bytes_accessed=cost * 3_000_000),
        )(*args)

    return run


def pairings(sectors, blocks):
    at = lambda a, r: (a % sectors) * blocks + r
    az0 = [(a, a ^ 1) for a in range(sectors)]
    az1 = [(a, (a + 1 if a % 2 else a - 1) % sectors) for a in range(sectors)]
    rad0 = [(r, r ^ 1) for r in range(blocks)]
    rad1 = []
    for a in range(sectors):
        for r in range(blocks):
            if r in (0, blocks - 1):
                rad1.append((at(a, r), at(a ^ 1, r)))
            else:
                rad1.append((at(a, r), at(a, r + 1 if r % 2 else r - 1)))
    return az0, az1, rad0, rad1


def shards(solution, metric, intersections, counts, projections):
    sectors, blocks = lax.axis_size("azim"), lax.axis_size("radax")
    az0, az1, rad0, rad1 = pairings(sectors, blocks)

    def across(r0, r1, s0, s1):
        gr1 = lax.ppermute(r1, ("azim", "radax"), rad1)
        gs1 = lax.ppermute(s1, "azim", az1)
        gr0 = lax.ppermute(r0, "radax", rad0)
        gs0 = lax.ppermute(s0, "azim", az0)
        return gs0, gs1, gr0, gr1

    state, rim, trace, first_trace = (2560, 128), (80, 128), (120, 128), (128, 128)
    dma = pltpu.SemaphoreType.DMA
    turned = jnp.concatenate([projections[:2], projections[2:].transpose(0, 1, 3, 2)], axis=0)
    tables = jnp.repeat(turned.transpose(1, 0, 2, 3).reshape(16, 64), 8, axis=1)
    tables = jnp.pad(tables, ((0, 112), (0, 0)))
    m = time_step * metric.transpose(3, 0, 1, 2).reshape(24, 128)
    nat, q = call(enter_kernel, [(8, 128, 320), state], [dma((8,))], {0: pltpu.HBM}, limit=50)(
        solution.reshape(8, 128, 320)
    )
    slots = intersections.transpose(0, 2, 1, 3)[0]
    (early,) = call(ahead_kernel, [state])(q, m, counts, slots)
    (s1,) = call(first_kernel, [first_trace])(counts, q, slots, early)
    (r1,) = call(rim_kernel, [rim])(nat, s1)
    (s0,) = call(others_kernel, [first_trace])(q, s1, r1)
    (r0,) = call(other_rim_kernel, [rim])(nat, s0)
    ga0, ga1, gr0, gr1 = across(r0, r1, s0, s1)
    (inner,) = call(inner_kernel, [state])(q, m, early)
    part, matrix, r1 = call(
        middle_kernel, [state, (64, 128), (136, 128)], [(64, 256), first_trace, first_trace]
    )(inner, q, m, s0, s1, tables, ga0, ga1)
    s, owed = call(block_kernel, [state, (1280, 128)], [rim, rim])(part, q, m, gr0, gr1)
    (s1,) = call(sector_kernel, [first_trace])(s)
    s0, r0 = call(later_kernel, [trace, (88, 128)])(s, part, m)
    got = across(r0, r1, s0, s1)
    (inner,) = call(inner_last_kernel, [state])(s, m, q)
    sides = [state, (64, 256), trace, trace, (88, 128), (88, 128)]
    (out,) = call(last_kernel, [(8, 128, 320)], sides + [(8, 128, 320), dma((24,))], {}, pltpu.HBM)(
        inner, s, m, s0, s1, matrix, owed, *got
    )
    return out.reshape(solution.shape)


def solution(mesh):
    in_specs = (
        P("azim", "radax", None, None),
        P("azim", "radax", None, None),
        P("azim", None, None, None),
        P("azim", None),
        P(),
    )
    out_specs = P("azim", "radax", None, None)
    return jax.shard_map(shards, mesh=mesh, in_specs=in_specs, out_specs=out_specs, check_vma=False)
```
